512 devices in a mesh: ctx: 128 (over y_lo, x, z), mp: 4 (over y_hi, core).
Axes of the slice: x: 4, y: 8 (y_hi: 2, y_lo: 4; y = y_hi * 4 + y_lo), z: 8, core: 2. Of those that a mesh axis runs over, the one named last changes fastest.
Arguments:
- query_rows: bfloat16 [16384, 2048], P('ctx', 'mp'), may hold values from -51 to 51
- key_rows: bfloat16 [16384, 2048], P('ctx', 'mp'), may hold values from -4 to 4
- value_rows: bfloat16 [16384, 2048], P('ctx', 'mp'), may hold values from -6 to 6
- inputs: bfloat16 [16384, 2048], P('ctx', 'mp'), may hold values from -3 to 3
- out_weight: bfloat16 [2048, 2048], P('mp'), may hold values from -0.125 to 0.125
- kernel: float32 [31, 2048], P(None, 'mp'), may hold values from -1 to 1
- cotangent: bfloat16 [16384, 2048], P('ctx', 'mp'), may hold values from -6 to 6
Outputs:
- output: bfloat16 [16384, 2048], P('ctx', 'mp')
- grad_input: bfloat16 [16384, 2048], P('ctx', 'mp')
- grad_query: bfloat16 [16384, 2048], P('ctx', 'mp')
- grad_key: bfloat16 [16384, 2048], P('ctx', 'mp')
- grad_value: bfloat16 [16384, 2048], P('ctx', 'mp')
The draws below stay inside these ranges and needn't reach their ends.
All inputs are finite; a program needn't handle non-finite values.
Results may differ from the reference program's by a relative error of at most 0.024.
Values may be sent and summed in bfloat16 or wider, within the bound.
A program may use at most 64 MiB of HBM per device.

```python
import math
import jax
import jax.numpy as jnp
from jax import lax

D = 2048
HEADS = 16
HDIM = 128
KS = 31
LOOK = 2
FR_DEV = 128
FRAMES = 16384


def band_pair(key):
    base_key = jax.random.fold_in(key, 11)
    first_key = jax.random.fold_in(base_key, 1)
    second_key = jax.random.fold_in(base_key, 2)
    key_vals = jnp.clip(jax.random.normal(first_key, (FRAMES, D), jnp.float32), -4.0, 4.0)
    query_vals = jnp.clip(3.0 * jax.random.normal(second_key, (FRAMES, D), jnp.float32), -12.0, 12.0)
    return (query_vals, key_vals)


def draw_query_rows(key, part):
    return band_pair(key)[0].astype(jnp.bfloat16)


def draw_key_rows(key, part):
    return band_pair(key)[1].astype(jnp.bfloat16)


def block_levels(own_key, shape, shards, least, top_value):
    gain = 1.0
    for axis_at, blocks in shards:
        draws = jax.random.uniform(jax.random.fold_in(jax.random.fold_in(own_key, 6), axis_at), (blocks,), jnp.float32, least / len(shards), top_value / len(shards))
        gain = gain * jnp.repeat(jnp.exp(draws), shape[axis_at] // blocks).reshape((-1,) + (1,) * (len(shape) - 1 - axis_at))
    return gain


def scatter_about(own_key, extent, spread, reach, cuts=(), held_as=jnp.bfloat16):
    entries = jax.random.normal(own_key, extent, jnp.float32) * spread
    if len(cuts) > 0:
        entries = block_levels(own_key, extent, cuts, -0.22, 0.18) * entries
    return jnp.clip(entries, min=-reach, max=reach).astype(held_as)


def setup_inputs(seed: int = 0) -> dict:
    streams_of = jax.random.split(jax.random.key(seed), 8)
    return {
        "query_rows": draw_query_rows(jax.random.fold_in(streams_of[7], 71), 0),
        "key_rows": draw_key_rows(jax.random.fold_in(streams_of[7], 71), 0),
        "value_rows": scatter_about(streams_of[2], (FRAMES, D), 1.0, 6.0, ((0, 128), (1, 4))),
        "inputs": scatter_about(streams_of[3], (FRAMES, D), 0.5, 3.0, ((0, 128), (1, 4))),
        "out_weight": scatter_about(streams_of[4], (D, D), D ** -0.5, 0.125, ((0, 4),)),
        "kernel": scatter_about(streams_of[5], (KS, D), KS ** -0.5, 1.0, ((1, 4),), jnp.float32),
        "cotangent": scatter_about(streams_of[6], (FRAMES, D), 1.0, 6.0, ((0, 128), (1, 4))),
    }


def split_heads(values_in):
    return values_in.astype(jnp.float32).reshape(values_in.shape[0], HEADS, HDIM)

def take_rows(values_in, row_start, length):
    return lax.dynamic_slice_in_dim(values_in, row_start, length, 0)

def reference(query_rows, key_rows, value_rows, inputs, out_weight, kernel, cotangent):
    score_scale = 1.0 / math.sqrt(HDIM)
    window_len = (2 * LOOK + 1) * FR_DEV
    margin = LOOK * FR_DEV
    blocks = FRAMES // FR_DEV

    def padded(values_in):
        return jnp.pad(values_in, ((margin, margin), (0, 0)))
    key_pad = padded(key_rows)
    value_pad = padded(value_rows)
    query_pad = padded(query_rows)

    def window_mask(block_index):
        owners = jnp.arange(window_len, dtype=jnp.int32) // FR_DEV - LOOK + block_index
        return (owners >= 0) & (owners < blocks)

    def forward_block(block_index):
        row_start = (block_index * FR_DEV).astype(jnp.int32)
        query_block = split_heads(take_rows(query_rows, row_start, FR_DEV))
        key_win = split_heads(take_rows(key_pad, row_start, window_len))
        value_win = split_heads(take_rows(value_pad, row_start, window_len))
        scores = jnp.einsum('qhd,khd->hqk', query_block, key_win) * score_scale
        scores = jnp.where(window_mask(block_index)[None, None, :], scores, -jnp.inf)
        row_max = lax.optimization_barrier(jnp.max(scores, axis=2))
        log_total = row_max + jnp.log(lax.optimization_barrier(jnp.sum(jnp.exp(scores - row_max[:, :, None]), axis=2)))
        probs_low = jnp.exp(scores - log_total[:, :, None]).astype(jnp.bfloat16)
        attended = jnp.einsum('hqk,khd->qhd', probs_low.astype(jnp.float32), value_win).astype(jnp.bfloat16)
        return (attended.reshape(FR_DEV, D), log_total)
    attended, log_parts = lax.map(forward_block, jnp.arange(blocks, dtype=jnp.int32))
    attended = attended.reshape(FRAMES, D)
    log_total = jnp.transpose(log_parts, (1, 0, 2)).reshape(HEADS, FRAMES)
    mixed = jnp.dot(attended, out_weight, preferred_element_type=jnp.float32)
    hidden = (inputs.astype(jnp.float32) + mixed).astype(jnp.bfloat16)
    half_kernel = KS // 2
    hidden_pad = jnp.pad(hidden.astype(jnp.float32), ((half_kernel, half_kernel), (0, 0)))
    conv_out = jnp.zeros((FRAMES, D), jnp.float32)
    for tap_index in range(KS):
        conv_out = conv_out + kernel[tap_index][None, :] * hidden_pad[tap_index:tap_index + FRAMES]
    conv_gate = jax.nn.sigmoid(conv_out)
    output = (hidden.astype(jnp.float32) + conv_out * conv_gate).astype(jnp.bfloat16)
    grad_conv = (cotangent.astype(jnp.float32) * (conv_gate + conv_out * conv_gate * (1.0 - conv_gate))).astype(jnp.bfloat16)
    grad_pad = jnp.pad(grad_conv.astype(jnp.float32), ((half_kernel, half_kernel), (0, 0)))
    grad_hidden = cotangent.astype(jnp.float32)
    for tap_index in range(KS):
        first_row = 2 * half_kernel - tap_index
        grad_hidden = grad_hidden + kernel[tap_index][None, :] * grad_pad[first_row:first_row + FRAMES]
    grad_input = grad_hidden.astype(jnp.bfloat16)
    upstream = jnp.dot(grad_input, out_weight.T, preferred_element_type=jnp.float32).astype(jnp.bfloat16)
    row_delta = lax.optimization_barrier(jnp.sum(split_heads(upstream) * split_heads(attended), axis=2)).T
    up_pad = padded(upstream)
    lse_pad = jnp.pad(log_total, ((0, 0), (margin, margin)))
    delta_pad = jnp.pad(row_delta, ((0, 0), (margin, margin)))

    def query_grad(block_index):
        row_start = (block_index * FR_DEV).astype(jnp.int32)
        query_block = split_heads(take_rows(query_rows, row_start, FR_DEV))
        up_block = split_heads(take_rows(upstream, row_start, FR_DEV))
        key_win = split_heads(take_rows(key_pad, row_start, window_len))
        value_win = split_heads(take_rows(value_pad, row_start, window_len))
        lse_block = lax.dynamic_slice_in_dim(log_total, row_start, FR_DEV, 1)
        delta_block = lax.dynamic_slice_in_dim(row_delta, row_start, FR_DEV, 1)
        scores = jnp.einsum('qhd,khd->hqk', query_block, key_win) * score_scale
        scores = jnp.where(window_mask(block_index)[None, None, :], scores, -jnp.inf)
        probs = jnp.exp(scores - lse_block[:, :, None])
        grad_dots = jnp.einsum('qhd,khd->hqk', up_block, value_win)
        grad_scores = (probs * (grad_dots - delta_block[:, :, None]) * score_scale).astype(jnp.bfloat16)
        result = jnp.einsum('hqk,khd->qhd', grad_scores.astype(jnp.float32), key_win)
        return result.astype(jnp.bfloat16).reshape(FR_DEV, D)

    def key_grad(block_index):
        row_start = (block_index * FR_DEV).astype(jnp.int32)
        key_block = split_heads(take_rows(key_rows, row_start, FR_DEV))
        value_block = split_heads(take_rows(value_rows, row_start, FR_DEV))
        query_win = split_heads(take_rows(query_pad, row_start, window_len))
        up_win = split_heads(take_rows(up_pad, row_start, window_len))
        lse_win = lax.dynamic_slice_in_dim(lse_pad, row_start, window_len, 1)
        delta_win = lax.dynamic_slice_in_dim(delta_pad, row_start, window_len, 1)
        valid = window_mask(block_index)[None, :, None]
        scores = jnp.einsum('qhd,khd->hqk', query_win, key_block) * score_scale
        probs = jnp.where(valid, jnp.exp(scores - lse_win[:, :, None]), 0.0)
        grad_value = jnp.einsum('hqk,qhd->khd', probs.astype(jnp.bfloat16).astype(jnp.float32), up_win)
        grad_dots = jnp.einsum('qhd,khd->hqk', up_win, value_block)
        grad_scores = (probs * (grad_dots - delta_win[:, :, None]) * score_scale).astype(jnp.bfloat16)
        grad_key = jnp.einsum('hqk,qhd->khd', grad_scores.astype(jnp.float32), query_win)
        return (grad_key.astype(jnp.bfloat16).reshape(FR_DEV, D), grad_value.astype(jnp.bfloat16).reshape(FR_DEV, D))
    grad_query = lax.map(query_grad, jnp.arange(blocks, dtype=jnp.int32)).reshape(FRAMES, D)
    grad_key, grad_value = lax.map(key_grad, jnp.arange(blocks, dtype=jnp.int32))
    return (output, grad_input, grad_query, grad_key.reshape(FRAMES, D), grad_value.reshape(FRAMES, D))
```

```python
import functools
import math

import jax
import jax.numpy as jnp
from jax import lax
from jax.experimental import pallas as pl
from jax.experimental.pallas import tpu as pltpu
from jax.sharding import PartitionSpec as P

HDIM = 128
LOOK = 2
BLOCKS = 2 * LOOK + 1
RIM = 32
HALF = 16
MESH = pl.DeviceIdType.MESH
F32 = jnp.float32
BF16 = jnp.bfloat16


def nt(a, b):
    return lax.dot_general(a, b, (((1,), (1,)), ((), ())), preferred_element_type=F32)


def nn(a, b):
    return jnp.dot(a, b, preferred_element_type=F32)


def kernel_body(
    count,
    heads,
    q_hbm,
    k_hbm,
    v_hbm,
    in_hbm,
    w_hbm,
    tap_hbm,
    cot_hbm,
    out_hbm,
    gi_hbm,
    gq_hbm,
    gk_hbm,
    gv_hbm,
    qwin,
    kwin,
    vwin,
    dowin,
    lsewin,
    deltawin,
    probs,
    probs_t,
    att,
    w_own,
    w_sib,
    taps,
    inp,
    cotp,
    own_sum,
    part_send,
    part_recv,
    rim_send,
    rim_own,
    rim_far,
    hpad,
    gpad,
    gfull,
    out_v,
    gq_v,
    gk_v,
    gv_v,
    local_sem,
    out_sem,
    kv_send,
    kv_recv,
    q_send,
    q_recv,
    lse_send,
    lse_recv,
    do_send,
    do_recv,
    delta_send,
    delta_recv,
    w_send,
    w_recv,
    cot_send,
    cot_recv,
    att_send,
    att_recv,
    part_ssem,
    part_rsem,
    rim_ssem,
    rim_rsem,
    gi_send,
    gi_recv,
):
    frames, width = inp.shape
    ntaps = taps.shape[0]
    scale = 1.0 / math.sqrt(HDIM)
    c = lax.axis_index("ctx")
    m = lax.axis_index("mp")
    right = lax.rem(c + 1, count)
    right2 = lax.rem(c + 2, count)
    left = lax.rem(c + count - 1, count)
    left2 = lax.rem(c + count - 2, count)
    sib_m = m + 1 - 2 * lax.rem(m, 2)
    far_m = lax.rem(m + 2, 4)
    far_sib_m = lax.rem(sib_m + 2, 4)
    sib = (c, sib_m)
    far = (c, far_m)

    barrier = pltpu.get_barrier_semaphore()
    partners = [
        (right, m), (left, m), (right2, m), (left2, m),
        sib, far, (right, far_m), (left, far_m),
    ]
    for device in partners:
        pl.semaphore_signal(barrier, inc=1, device_id=device, device_id_type=MESH)

    def local(src, dst, at):
        copy = pltpu.make_async_copy(src, dst, local_sem.at[at])
        copy.start()
        return copy

    def remote(src, dst, send, recv, device):
        return pltpu.make_async_remote_copy(
            src_ref=src, dst_ref=dst, send_sem=send, recv_sem=recv,
            device_id=device, device_id_type=MESH,
        )

    def cols(index):
        return slice(index * HDIM, (index + 1) * HDIM)

    def block(slot):
        return slice(slot * frames, (slot + 1) * frames)

    def wide(index):
        return pl.ds(pl.multiple_of(index * width, width), width)

    mid = block(LOOK)
    loads = {}
    for h in range(heads):
        loads["q", h] = local(q_hbm.at[:, cols(h)], qwin.at[h, mid], h)
        loads["k", h] = local(k_hbm.at[:, cols(h)], kwin.at[h, mid], heads + h)
        loads["v", h] = local(v_hbm.at[:, cols(h)], vwin.at[h, mid], 2 * heads + h)
    at = 3 * heads
    loads["w"] = local(w_hbm, w_own, at)
    loads["taps"] = local(tap_hbm, taps, at + 1)
    loads["inp"] = local(in_hbm, inp, at + 2)
    loads["cot"] = local(cot_hbm, cotp.at[HALF : HALF + frames], at + 3)

    pl.semaphore_wait(barrier, len(partners))

    first = {}
    second = {}
    for h in range(heads):
        for i, (src, win) in enumerate(((k_hbm, kwin), (v_hbm, vwin))):
            first[h, i, 0] = remote(
                src.at[:, cols(h)], win.at[h, block(1)], kv_send.at[0, i, h], kv_recv.at[0, i, h], (right, m)
            )
            first[h, i, 1] = remote(
                src.at[:, cols(h)], win.at[h, block(3)], kv_send.at[1, i, h], kv_recv.at[1, i, h], (left, m)
            )
            first[h, i, 0].start()
            first[h, i, 1].start()
            second[h, i, 0] = remote(
                win.at[h, block(1)], win.at[h, block(0)], kv_send.at[2, i, h], kv_recv.at[2, i, h], (right, m)
            )
            second[h, i, 1] = remote(
                win.at[h, block(3)], win.at[h, block(4)], kv_send.at[3, i, h], kv_recv.at[3, i, h], (left, m)
            )

    early = [
        remote(w_hbm.at[:, wide(sib_m)], w_sib.at[0], w_send.at[0], w_recv.at[0], sib),
        remote(w_hbm.at[:, wide(far_sib_m)], w_sib.at[1], w_send.at[1], w_recv.at[1], sib),
        remote(
            cot_hbm.at[frames - HALF : frames], cotp.at[0:HALF], cot_send.at[0], cot_recv.at[0], (right, m)
        ),
        remote(
            cot_hbm.at[0:HALF],
            cotp.at[HALF + frames : 2 * HALF + frames],
            cot_send.at[1],
            cot_recv.at[1],
            (left, m),
        ),
    ]
    for copy in early:
        copy.start()

    for h in range(heads):
        for side in range(2):
            for i in range(2):
                first[h, i, side].wait_recv()
                second[h, i, side].start()

    owner = lax.shift_right_logical(
        lax.broadcasted_iota(jnp.int32, (1, BLOCKS * frames), 1), 7
    ) + c
    valid = (owner >= LOOK) & (owner < count + LOOK)
    lane = lax.broadcasted_iota(jnp.int32, (frames, HDIM), 1)

    stat = jnp.zeros((frames, HDIM), F32)
    shares = []
    for h in range(heads):
        loads["q", h].wait()
        loads["k", h].wait()
        loads["v", h].wait()
        for side in range(2):
            for i in range(2):
                second[h, i, side].wait_recv()
        scores = nt(qwin[h, mid], kwin[h]) * scale
        scores = jnp.where(valid, scores, -jnp.inf)
        top = jnp.max(scores, axis=1, keepdims=True)
        weights = jnp.exp(scores - top)
        total = jnp.sum(weights, axis=1, keepdims=True)
        stat = jnp.where(lane == h, top + jnp.log(total), stat)
        prob = weights * (1.0 / total)
        probs[h] = prob
        att[0, :, cols(h)] = nn(prob.astype(BF16), vwin[h]).astype(BF16)
        share = remote(att.at[0, :, cols(h)], att.at[1, :, cols(h)], att_send.at[h], att_recv.at[h], sib)
        share.start()
        shares.append(share)
    lsewin[:, mid] = jnp.transpose(stat)[0:8]

    loads["w"].wait()
    far_part = nn(att[0], w_own[:, wide(far_m)])
    own_part = nn(att[0], w_own[:, wide(m)])
    early[0].wait_recv()
    early[1].wait_recv()
    for share in shares:
        share.wait_recv()
    part_send[...] = (far_part + nn(att[1], w_sib[1])).astype(BF16)
    parts = [
        remote(part_send, part_recv, part_ssem, part_rsem, far),
        remote(
            part_send.at[frames - RIM : frames], rim_far.at[0], rim_ssem.at[0], rim_rsem.at[0], (right, far_m)
        ),
        remote(part_send.at[0:RIM], rim_far.at[1], rim_ssem.at[1], rim_rsem.at[1], (left, far_m)),
    ]
    for copy in parts:
        copy.start()
    loads["inp"].wait()
    summed = own_part + nn(att[1], w_sib[0]) + inp[...].astype(F32)
    own_sum[...] = summed
    rim_send[0] = summed[frames - RIM : frames].astype(BF16)
    rim_send[1] = summed[0:RIM].astype(BF16)
    rims = [
        remote(rim_send.at[0], rim_own.at[0], rim_ssem.at[2], rim_rsem.at[2], (right, m)),
        remote(rim_send.at[1], rim_own.at[1], rim_ssem.at[3], rim_rsem.at[3], (left, m)),
    ]
    for copy in rims:
        copy.start()

    routes = [((right, m), 1), ((left, m), 3), ((right2, m), 0), ((left2, m), 4)]
    queries = []
    for i, (device, slot) in enumerate(routes):
        queries.append(
            remote(qwin.at[:, mid], qwin.at[:, block(slot)], q_send.at[i], q_recv.at[i], device)
        )
        queries.append(
            remote(lsewin.at[:, mid], lsewin.at[:, block(slot)], lse_send.at[i], lse_recv.at[i], device)
        )
    for copy in queries:
        copy.start()

    loads["taps"].wait()
    loads["cot"].wait()
    early[2].wait_recv()
    early[3].wait_recv()
    for copy in parts + rims:
        copy.wait_recv()

    row = lax.broadcasted_iota(jnp.int32, (frames + 2 * HALF, HDIM), 0)
    inside = ((row >= HALF) | (c > 0)) & ((row < HALF + frames) | (c < count - 1))
    spread = []
    for j in range(width // HDIM):
        lanes = cols(j)
        hidden = (own_sum[:, lanes] + part_recv[:, lanes].astype(F32)).astype(BF16).astype(F32)
        hpad[j, RIM : RIM + frames] = hidden
        low = (rim_own[0, :, lanes].astype(F32) + rim_far[0, :, lanes].astype(F32)).astype(BF16).astype(F32)
        high = (rim_own[1, :, lanes].astype(F32) + rim_far[1, :, lanes].astype(F32)).astype(BF16).astype(F32)
        hpad[j, 0:RIM] = jnp.where(c > 0, low, 0.0)
        hpad[j, RIM + frames : 2 * RIM + frames] = jnp.where(c < count - 1, high, 0.0)
        conv = jnp.zeros((frames + 2 * HALF, HDIM), F32)
        for tap in range(ntaps):
            conv = conv + taps[tap : tap + 1, lanes] * hpad[j, tap + 1 : tap + 1 + frames + 2 * HALF]
        gate = jax.nn.sigmoid(conv)
        swish = conv * gate
        out_v[:, lanes] = (hidden + swish[HALF : HALF + frames]).astype(BF16)
        cot = cotp[:, lanes].astype(F32)
        grad_conv = (cot * (gate + swish * (1.0 - gate))).astype(BF16).astype(F32)
        gpad[j] = jnp.where(inside, grad_conv, 0.0)
        grad = cot[HALF : HALF + frames]
        for tap in range(ntaps):
            start = 2 * HALF - 1 - tap
            grad = grad + taps[tap : tap + 1, lanes] * gpad[j, start : start + frames]
        gfull[0, :, lanes] = grad.astype(BF16)
        to_sib = remote(gfull.at[0, :, lanes], gfull.at[1, :, lanes], gi_send.at[0, j], gi_recv.at[0, j], sib)
        to_far = remote(gfull.at[0, :, lanes], gfull.at[2, :, lanes], gi_send.at[1, j], gi_recv.at[1, j], far)
        relay = remote(gfull.at[2, :, lanes], gfull.at[3, :, lanes], gi_send.at[2, j], gi_recv.at[2, j], sib)
        to_far.start()
        to_sib.start()
        spread.append((to_sib, to_far, relay))

    stores = [
        pltpu.make_async_copy(out_v, out_hbm, out_sem.at[0]),
        pltpu.make_async_copy(gfull.at[0], gi_hbm, out_sem.at[1]),
    ]
    for copy in stores:
        copy.start()

    for copy in queries:
        copy.wait_recv()
    for h in range(heads):
        scores_t = nt(kwin[h, mid], qwin[h]) * scale
        probs_t[h] = jnp.where(valid, jnp.exp(scores_t - lsewin[h : h + 1]), 0.0)

    up = nt(gfull[0], w_own[:, wide(m)])
    for to_sib, to_far, relay in spread:
        to_far.wait_recv()
        relay.start()
    for to_sib, to_far, relay in spread:
        to_sib.wait_recv()
    up = up + nt(gfull[1], w_own[:, wide(sib_m)])
    up = up + nt(gfull[2], w_own[:, wide(far_m)])
    for to_sib, to_far, relay in spread:
        relay.wait_recv()
    up = up + nt(gfull[3], w_own[:, wide(far_sib_m)])
    upstream = up.astype(BF16)

    delta = []
    stat = jnp.zeros((frames, HDIM), F32)
    for h in range(heads):
        part = upstream[:, cols(h)]
        dowin[h, mid] = part
        delta.append(
            jnp.sum(part.astype(F32) * att[0, :, cols(h)].astype(F32), axis=1, keepdims=True)
        )
        stat = jnp.where(lane == h, delta[h], stat)
    deltawin[:, mid] = jnp.transpose(stat)[0:8]
    ups = []
    for i, (device, slot) in enumerate(routes):
        ups.append(
            remote(dowin.at[:, mid], dowin.at[:, block(slot)], do_send.at[i], do_recv.at[i], device)
        )
        ups.append(
            remote(deltawin.at[:, mid], deltawin.at[:, block(slot)], delta_send.at[i], delta_recv.at[i], device)
        )
    for copy in ups:
        copy.start()

    for h in range(heads):
        dots = nt(dowin[h, mid], vwin[h])
        grad_scores = (probs[h] * (dots - delta[h]) * scale).astype(BF16)
        gq_v[:, cols(h)] = nn(grad_scores, kwin[h]).astype(BF16)
    stores.append(pltpu.make_async_copy(gq_v, gq_hbm, out_sem.at[2]))
    stores[-1].start()

    for copy in ups:
        copy.wait_recv()
    for h in range(heads):
        prob_t = probs_t[h]
        gv_v[:, cols(h)] = nn(prob_t.astype(BF16), dowin[h]).astype(BF16)
        dots_t = nt(vwin[h, mid], dowin[h])
        grad_t = (prob_t * (dots_t - deltawin[h : h + 1]) * scale).astype(BF16)
        gk_v[:, cols(h)] = nn(grad_t, qwin[h]).astype(BF16)
    stores.append(pltpu.make_async_copy(gk_v, gk_hbm, out_sem.at[3]))
    stores[-1].start()
    stores.append(pltpu.make_async_copy(gv_v, gv_hbm, out_sem.at[4]))
    stores[-1].start()

    for copy in list(first.values()) + list(second.values()) + early + shares + parts + rims + queries + ups:
        copy.wait_send()
    for group in spread:
        for copy in group:
            copy.wait_send()
    for copy in stores:
        copy.wait()


def per_device(query_rows, key_rows, value_rows, inputs, out_weight, kernel, cotangent):
    frames, width = query_rows.shape
    heads = width // HDIM
    count = lax.axis_size("ctx")
    window = BLOCKS * frames
    full = out_weight.shape[1]
    chunks = width // HDIM
    taps = kernel.shape[0]
    dma = pltpu.SemaphoreType.DMA
    win = pltpu.VMEM((heads, window, HDIM), BF16)
    scratch = [
        win, win, win, win,
        pltpu.VMEM((8, window), F32),
        pltpu.VMEM((8, window), F32),
        pltpu.VMEM((heads, frames, window), F32),
        pltpu.VMEM((heads, frames, window), F32),
        pltpu.VMEM((2, frames, width), BF16),
        pltpu.VMEM((width, full), BF16),
        pltpu.VMEM((2, width, width), BF16),
        pltpu.VMEM((taps, width), F32),
        pltpu.VMEM((frames, width), BF16),
        pltpu.VMEM((frames + 2 * HALF, width), BF16),
        pltpu.VMEM((frames, width), F32),
        pltpu.VMEM((frames, width), BF16),
        pltpu.VMEM((frames, width), BF16),
        pltpu.VMEM((2, RIM, width), BF16),
        pltpu.VMEM((2, RIM, width), BF16),
        pltpu.VMEM((2, RIM, width), BF16),
        pltpu.VMEM((chunks, frames + 2 * RIM, HDIM), F32),
        pltpu.VMEM((chunks, frames + 2 * HALF, HDIM), F32),
        pltpu.VMEM((4, frames, width), BF16),
        pltpu.VMEM((frames, width), BF16),
        pltpu.VMEM((frames, width), BF16),
        pltpu.VMEM((frames, width), BF16),
        pltpu.VMEM((frames, width), BF16),
        dma((3 * heads + 4,)),
        dma((5,)),
        dma((4, 2, heads)), dma((4, 2, heads)),
        dma((4,)), dma((4,)),
        dma((4,)), dma((4,)),
        dma((4,)), dma((4,)),
        dma((4,)), dma((4,)),
        dma((2,)), dma((2,)),
        dma((2,)), dma((2,)),
        dma((heads,)), dma((heads,)),
        dma, dma,
        dma((4,)), dma((4,)),
        dma((3, chunks)), dma((3, chunks)),
    ]
    shape = jax.ShapeDtypeStruct((frames, width), BF16)
    return pl.pallas_call(
        functools.partial(kernel_body, count, heads),
        out_shape=(shape,) * 5,
        in_specs=[pl.BlockSpec(memory_space=pl.ANY)] * 7,
        out_specs=(pl.BlockSpec(memory_space=pl.ANY),) * 5,
        scratch_shapes=scratch,
        compiler_params=pltpu.CompilerParams(
            collective_id=0, has_side_effects=True, vmem_limit_bytes=56 * 1024 * 1024
        ),
        name="conformer",
    )(query_rows, key_rows, value_rows, inputs, out_weight, kernel, cotangent)


def solution(mesh):
    placed = (
        P("ctx", "mp"),
        P("ctx", "mp"),
        P("ctx", "mp"),
        P("ctx", "mp"),
        P("mp", None),
        P(None, "mp"),
        P("ctx", "mp"),
    )
    return jax.shard_map(
        per_device,
        mesh=mesh,
        in_specs=placed,
        out_specs=(P("ctx", "mp"),) * 5,
        check_vma=False,
    )
```

```python
import functools
import math

import jax
import jax.numpy as jnp
from jax import lax
from jax.experimental import pallas as pl
from jax.experimental.pallas import tpu as pltpu
from jax.sharding import PartitionSpec as P

HDIM = 128
LOOK = 2
BLOCKS = 2 * LOOK + 1
RIM = 32
HALF = 16
MESH = pl.DeviceIdType.MESH
F32 = jnp.float32
BF16 = jnp.bfloat16


def nt(a, b):
    return lax.dot_general(a, b, (((1,), (1,)), ((), ())), preferred_element_type=F32)


def nn(a, b):
    return jnp.dot(a, b, preferred_element_type=F32)


def kernel_body(
    count,
    heads,
    q_hbm,
    k_hbm,
    v_hbm,
    in_hbm,
    w_hbm,
    tap_hbm,
    cot_hbm,
    out_hbm,
    gi_hbm,
    gq_hbm,
    gk_hbm,
    gv_hbm,
    qwin,
    kwin,
    vwin,
    dowin,
    lsewin,
    deltawin,
    probs,
    probs_t,
    att,
    w_own,
    w_sib,
    taps,
    inp,
    cotp,
    own_sum,
    part_send,
    part_recv,
    rim_send,
    rim_own,
    rim_far,
    hpad,
    gpad,
    gfull,
    out_v,
    gq_v,
    gk_v,
    gv_v,
    gk_sum,
    gv_sum,
    local_sem,
    out_sem,
    kv_send,
    kv_recv,
    q_send,
    q_recv,
    lse_send,
    lse_recv,
    do_send,
    do_recv,
    delta_send,
    delta_recv,
    w_send,
    w_recv,
    cot_send,
    cot_recv,
    att_send,
    att_recv,
    part_ssem,
    part_rsem,
    rim_ssem,
    rim_rsem,
    gi_send,
    gi_recv,
):
    frames, width = inp.shape
    ntaps = taps.shape[0]
    scale = 1.0 / math.sqrt(HDIM)
    c = lax.axis_index("ctx")
    m = lax.axis_index("mp")
    right = lax.rem(c + 1, count)
    right2 = lax.rem(c + 2, count)
    left = lax.rem(c + count - 1, count)
    left2 = lax.rem(c + count - 2, count)
    sib_m = m + 1 - 2 * lax.rem(m, 2)
    far_m = lax.rem(m + 2, 4)
    far_sib_m = lax.rem(sib_m + 2, 4)
    sib = (c, sib_m)
    far = (c, far_m)

    barrier = pltpu.get_barrier_semaphore()
    exists = [c < count - 1, c > 0, c < count - 2, c > 1]
    targets = [right, left, right2, left2]
    places = [1, 3, 0, 4]

    def toward(i, plane=None):
        other = sib_m if plane is None else plane
        own = m if plane is None else plane
        return (jnp.where(exists[i], targets[i], c), jnp.where(exists[i], own, other))

    def turned(i, value, mirrored):
        return jnp.where(exists[i], value, mirrored)

    def place(i, slot):
        return pl.ds(pl.multiple_of(turned(i, slot, 4 - slot) * frames, frames), frames)

    partners = [toward(i) for i in range(4)] + [sib, far, toward(0, far_m), toward(1, far_m)]
    for device in partners:
        pl.semaphore_signal(barrier, inc=1, device_id=device, device_id_type=MESH)

    def local(src, dst, at):
        copy = pltpu.make_async_copy(src, dst, local_sem.at[at])
        copy.start()
        return copy

    def remote(src, dst, send, recv, device):
        return pltpu.make_async_remote_copy(
            src_ref=src, dst_ref=dst, send_sem=send, recv_sem=recv,
            device_id=device, device_id_type=MESH,
        )

    class Crossing:
        def __init__(self, sent, due):
            self.start, self.wait_send, self.wait_recv = sent.start, sent.wait_send, due.wait_recv

    def shift(src, dst, due_dst, send, recv, due_recv, device):
        return Crossing(
            remote(src, dst, send, recv, device), remote(src, due_dst, send, due_recv, device)
        )

    def cols(index):
        return slice(index * HDIM, (index + 1) * HDIM)

    def block(slot):
        return slice(slot * frames, (slot + 1) * frames)

    def wide(index):
        return pl.ds(pl.multiple_of(index * width, width), width)

    mid = block(LOOK)
    loads = {}
    for h in range(heads):
        loads["q", h] = local(q_hbm.at[:, cols(h)], qwin.at[h, mid], h)
        loads["k", h] = local(k_hbm.at[:, cols(h)], kwin.at[h, mid], heads + h)
        loads["v", h] = local(v_hbm.at[:, cols(h)], vwin.at[h, mid], 2 * heads + h)
    at = 3 * heads
    loads["w"] = local(w_hbm, w_own, at)
    loads["taps"] = local(tap_hbm, taps, at + 1)
    loads["inp"] = local(in_hbm, inp, at + 2)
    loads["cot"] = local(cot_hbm, cotp.at[HALF : HALF + frames], at + 3)

    pl.semaphore_wait(barrier, len(partners))

    first = {}
    second = {}
    for h in range(heads):
        for i, (src, win) in enumerate(((k_hbm, kwin), (v_hbm, vwin))):
            for side in range(2):
                near_slot, far_slot = places[side], places[2 + side]
                first[h, i, side] = shift(
                    src.at[:, cols(h)], win.at[h, place(side, near_slot)], win.at[h, block(near_slot)],
                    kv_send.at[side, i, h], kv_recv.at[turned(side, side, 1 - side), i, h],
                    kv_recv.at[side, i, h], toward(side),
                )
                first[h, i, side].start()
                second[h, i, side] = shift(
                    win.at[h, block(near_slot)], win.at[h, place(side, far_slot)], win.at[h, block(far_slot)],
                    kv_send.at[2 + side, i, h], kv_recv.at[2 + turned(side, side, 1 - side), i, h],
                    kv_recv.at[2 + side, i, h], toward(side),
                )

    early = [
        remote(w_hbm.at[:, wide(sib_m)], w_sib.at[0], w_send.at[0], w_recv.at[0], sib),
        remote(w_hbm.at[:, wide(far_sib_m)], w_sib.at[1], w_send.at[1], w_recv.at[1], sib),
    ]
    cot_starts = (0, HALF + frames)
    for side, rows in enumerate((slice(frames - HALF, frames), slice(0, HALF))):
        start = turned(side, cot_starts[side], cot_starts[1 - side])
        early.append(shift(
            cot_hbm.at[rows], cotp.at[pl.ds(pl.multiple_of(start, HALF), HALF)],
            cotp.at[cot_starts[side] : cot_starts[side] + HALF],
            cot_send.at[side], cot_recv.at[turned(side, side, 1 - side)], cot_recv.at[side], toward(side),
        ))
    for copy in early:
        copy.start()

    for h in range(heads):
        for side in range(2):
            for i in range(2):
                first[h, i, side].wait_recv()
                second[h, i, side].start()

    owner = lax.shift_right_logical(
        lax.broadcasted_iota(jnp.int32, (1, BLOCKS * frames), 1), 7
    ) + c
    valid = (owner >= LOOK) & (owner < count + LOOK)
    lane = lax.broadcasted_iota(jnp.int32, (frames, HDIM), 1)

    def spread_to(i, win, send, recv, source=mid):
        return shift(
            win.at[:, source], win.at[:, place(i, places[i])], win.at[:, block(places[i])],
            send.at[i], recv.at[turned(i, i, i ^ 1)], recv.at[i], toward(i),
        )

    def relay_to(side, win, send, recv):
        near_slot, far_slot = places[side], places[2 + side]
        return shift(
            win.at[:, block(near_slot)], win.at[:, place(side, far_slot)], win.at[:, block(far_slot)],
            send.at[2 + side], recv.at[2 + turned(side, side, 1 - side)], recv.at[2 + side], toward(side),
        )

    queries = [spread_to(side, qwin, q_send, q_recv) for side in range(2)]
    queries += [relay_to(side, qwin, q_send, q_recv) for side in range(2)]

    stat = jnp.zeros((frames, HDIM), F32)
    shares = []
    for h in range(heads):
        loads["q", h].wait()
        loads["k", h].wait()
        loads["v", h].wait()
        for side in range(2):
            for i in range(2):
                second[h, i, side].wait_recv()
        if h == heads - 1:
            queries[0].start()
            queries[1].start()
        scores = nt(qwin[h, mid], kwin[h]) * scale
        scores = jnp.where(valid, scores, -jnp.inf)
        top = jnp.max(scores, axis=1, keepdims=True)
        weights = jnp.exp(scores - top)
        total = jnp.sum(weights, axis=1, keepdims=True)
        stat = jnp.where(lane == h, top + jnp.log(total), stat)
        prob = weights * (1.0 / total)
        probs[h] = prob
        att[0, :, cols(h)] = nn(prob.astype(BF16), vwin[h]).astype(BF16)
        share = remote(att.at[0, :, cols(h)], att.at[1, :, cols(h)], att_send.at[h], att_recv.at[h], sib)
        share.start()
        shares.append(share)
    lsewin[:, mid] = jnp.transpose(stat)[0:8]

    loads["w"].wait()
    early[0].wait_recv()
    early[1].wait_recv()
    for share in shares:
        share.wait_recv()
    parts = []
    for j in range(width // HDIM):
        lanes = cols(j)
        far_cols = pl.ds(pl.multiple_of(far_m * width + j * HDIM, HDIM), HDIM)
        part_send[:, lanes] = (nn(att[0], w_own[:, far_cols]) + nn(att[1], w_sib[1, :, lanes])).astype(BF16)
        group = [
            remote(part_send.at[:, lanes], part_recv.at[:, lanes], part_ssem.at[j], part_rsem.at[j], far)
        ]
        for side, rows in enumerate((slice(frames - RIM, frames), slice(0, RIM))):
            turn = turned(side, side, 1 - side)
            group.append(shift(
                part_send.at[rows, lanes], rim_far.at[turn, :, lanes], rim_far.at[side, :, lanes],
                rim_ssem.at[side, j], rim_rsem.at[turn, j], rim_rsem.at[side, j], toward(side, far_m),
            ))
        for copy in group:
            copy.start()
        parts.append(group)
    loads["inp"].wait()
    own_part = nn(att[0], w_own[:, wide(m)])
    summed = own_part + nn(att[1], w_sib[0]) + inp[...].astype(F32)
    own_sum[...] = summed

    rims = []
    rim_send[0] = summed[frames - RIM : frames].astype(BF16)
    rim_send[1] = summed[0:RIM].astype(BF16)
    for j in range(width // HDIM):
        lanes = cols(j)
        pair = []
        for side in range(2):
            turn = turned(side, side, 1 - side)
            pair.append(shift(
                rim_send.at[side, :, lanes], rim_own.at[turn, :, lanes], rim_own.at[side, :, lanes],
                rim_ssem.at[2 + side, j], rim_rsem.at[2 + turn, j], rim_rsem.at[2 + side, j], toward(side),
            ))
            pair[-1].start()
        rims.append(pair)

    for side in range(2):
        queries[side].wait_recv()
        queries[2 + side].start()
    totals = [spread_to(i, lsewin, lse_send, lse_recv) for i in range(4)]
    for copy in totals:
        copy.start()

    loads["taps"].wait()
    loads["cot"].wait()
    early[2].wait_recv()
    early[3].wait_recv()

    row = lax.broadcasted_iota(jnp.int32, (frames + 2 * HALF, HDIM), 0)
    inside = ((row >= HALF) | (c > 0)) & ((row < HALF + frames) | (c < count - 1))
    spread = []

    def take(j):
        lanes = cols(j)
        for copy in parts[j]:
            copy.wait_recv()
        hidden = (own_sum[:, lanes] + part_recv[:, lanes].astype(F32)).astype(BF16)
        hpad[j, RIM : RIM + frames] = hidden.astype(F32)

    take(0)
    for j in range(width // HDIM):
        if j + 1 < width // HDIM:
            take(j + 1)
        lanes = cols(j)
        for copy in rims[j]:
            copy.wait_recv()
        low = (rim_own[0, :, lanes].astype(F32) + rim_far[0, :, lanes].astype(F32)).astype(BF16).astype(F32)
        high = (rim_own[1, :, lanes].astype(F32) + rim_far[1, :, lanes].astype(F32)).astype(BF16).astype(F32)
        hpad[j, 0:RIM] = jnp.where(c > 0, low, 0.0)
        hpad[j, RIM + frames : 2 * RIM + frames] = jnp.where(c < count - 1, high, 0.0)
        conv = jnp.zeros((frames + 2 * HALF, HDIM), F32)
        for tap in range(ntaps):
            conv = conv + taps[tap : tap + 1, lanes] * hpad[j, tap + 1 : tap + 1 + frames + 2 * HALF]
        gate = jax.nn.sigmoid(conv)
        swish = conv * gate
        out_v[:, lanes] = (hpad[j, RIM : RIM + frames] + swish[HALF : HALF + frames]).astype(BF16)
        cot = cotp[:, lanes].astype(F32)
        grad_conv = (cot * (gate + swish * (1.0 - gate))).astype(BF16).astype(F32)
        gpad[j] = jnp.where(inside, grad_conv, 0.0)
        grad = cot[HALF : HALF + frames]
        for tap in range(ntaps):
            start = 2 * HALF - 1 - tap
            grad = grad + taps[tap : tap + 1, lanes] * gpad[j, start : start + frames]
        gfull[0, :, lanes] = grad.astype(BF16)
        to_sib = remote(gfull.at[0, :, lanes], gfull.at[1, :, lanes], gi_send.at[0, j], gi_recv.at[0, j], sib)
        to_far = remote(gfull.at[0, :, lanes], gfull.at[2, :, lanes], gi_send.at[1, j], gi_recv.at[1, j], far)
        relay = remote(gfull.at[2, :, lanes], gfull.at[3, :, lanes], gi_send.at[2, j], gi_recv.at[2, j], sib)
        to_far.start()
        to_sib.start()
        spread.append((to_sib, to_far, relay))

    stores = [
        pltpu.make_async_copy(out_v, out_hbm, out_sem.at[0]),
        pltpu.make_async_copy(gfull.at[0], gi_hbm, out_sem.at[1]),
    ]
    for copy in stores:
        copy.start()

    for copy in queries[2:] + totals:
        copy.wait_recv()
    for h in range(heads):
        scores_t = nt(kwin[h, mid], qwin[h]) * scale
        probs_t[h] = jnp.where(valid, jnp.exp(scores_t - lsewin[h : h + 1]), 0.0)

    up = nt(gfull[0], w_own[:, wide(m)])
    for to_sib, to_far, relay in spread:
        to_far.wait_recv()
        relay.start()
    for to_sib, to_far, relay in spread:
        to_sib.wait_recv()
    up = up + nt(gfull[1], w_own[:, wide(sib_m)])
    up = up + nt(gfull[2], w_own[:, wide(far_m)])
    for to_sib, to_far, relay in spread:
        relay.wait_recv()
    up = up + nt(gfull[3], w_own[:, wide(far_sib_m)])
    upstream = up.astype(BF16)

    delta = []
    stat = jnp.zeros((frames, HDIM), F32)
    for h in range(heads):
        part = upstream[:, cols(h)]
        dowin[h, mid] = part
        delta.append(
            jnp.sum(part.astype(F32) * att[0, :, cols(h)].astype(F32), axis=1, keepdims=True)
        )
        stat = jnp.where(lane == h, delta[h], stat)
    deltawin[:, mid] = jnp.transpose(stat)[0:8]
    ups = []
    second_ups = []
    for h in range(heads):
        for side in range(2):
            turn = turned(side, side, 1 - side)
            near_slot, far_slot = places[side], places[2 + side]
            ups.append(shift(
                dowin.at[h, mid], dowin.at[h, place(side, near_slot)], dowin.at[h, block(near_slot)],
                do_send.at[side, h], do_recv.at[turn, h], do_recv.at[side, h], toward(side),
            ))
            ups[-1].start()
            second_ups.append(shift(
                dowin.at[h, block(near_slot)], dowin.at[h, place(side, far_slot)], dowin.at[h, block(far_slot)],
                do_send.at[2 + side, h], do_recv.at[2 + turn, h], do_recv.at[2 + side, h], toward(side),
            ))
    deltas = [spread_to(i, deltawin, delta_send, delta_recv) for i in range(4)]
    for copy in deltas:
        copy.start()

    def query_grad(h):
        dots = nt(dowin[h, mid], vwin[h])
        grad_scores = (probs[h] * (dots - delta[h]) * scale).astype(BF16)
        gq_v[:, cols(h)] = nn(grad_scores, kwin[h]).astype(BF16)

    def key_grad(h, span):
        prob_t = probs_t[h, :, span]
        d_value = nn(prob_t.astype(BF16), dowin[h, span])
        dots_t = nt(vwin[h, mid], dowin[h, span])
        grad_t = (prob_t * (dots_t - deltawin[h : h + 1, span]) * scale).astype(BF16)
        return nn(grad_t, qwin[h, span]), d_value

    for h in range(heads):
        query_grad(h)
    stores.append(pltpu.make_async_copy(gq_v, gq_hbm, out_sem.at[2]))
    stores[-1].start()
    for one, two in zip(ups, second_ups):
        one.wait_recv()
        two.start()
    for copy in deltas:
        copy.wait_recv()
    near = slice(frames, 4 * frames)
    for h in range(heads):
        gk_sum[:, cols(h)], gv_sum[:, cols(h)] = key_grad(h, near)
    for h in range(heads):
        for side in range(2):
            second_ups[2 * h + side].wait_recv()
        low_k, low_v = key_grad(h, block(0))
        high_k, high_v = key_grad(h, block(4))
        gk_v[:, cols(h)] = (gk_sum[:, cols(h)] + low_k + high_k).astype(BF16)
        gv_v[:, cols(h)] = (gv_sum[:, cols(h)] + low_v + high_v).astype(BF16)
    stores.append(pltpu.make_async_copy(gk_v, gk_hbm, out_sem.at[3]))
    stores[-1].start()
    stores.append(pltpu.make_async_copy(gv_v, gv_hbm, out_sem.at[4]))
    stores[-1].start()

    for copy in list(first.values()) + list(second.values()) + early + shares + queries + totals:
        copy.wait_send()
    for copy in ups + second_ups + deltas:
        copy.wait_send()
    for group in parts + rims + spread:
        for copy in group:
            copy.wait_send()
    for copy in stores:
        copy.wait()


def copy_out(*refs):
    sources, targets, held, sems = refs[:5], refs[5:10], refs[10], refs[11]
    taken = [pltpu.make_async_copy(source, held.at[i], sems.at[0, i]) for i, source in enumerate(sources)]
    given = [pltpu.make_async_copy(held.at[i], target, sems.at[1, i]) for i, target in enumerate(targets)]
    for copy in taken:
        copy.start()
    for one, two in zip(taken, given):
        one.wait()
        two.start()
    for copy in given:
        copy.wait()


def per_device(query_rows, key_rows, value_rows, inputs, out_weight, kernel, cotangent):
    frames, width = query_rows.shape
    heads = width // HDIM
    count = lax.axis_size("ctx")
    window = BLOCKS * frames
    full = out_weight.shape[1]
    chunks = width // HDIM
    taps = kernel.shape[0]
    dma = pltpu.SemaphoreType.DMA
    win = pltpu.VMEM((heads, window, HDIM), BF16)
    scratch = [
        win, win, win, win,
        pltpu.VMEM((8, window), F32),
        pltpu.VMEM((8, window), F32),
        pltpu.VMEM((heads, frames, window), F32),
        pltpu.VMEM((heads, frames, window), F32),
        pltpu.VMEM((2, frames, width), BF16),
        pltpu.VMEM((width, full), BF16),
        pltpu.VMEM((2, width, width), BF16),
        pltpu.VMEM((taps, width), F32),
        pltpu.VMEM((frames, width), BF16),
        pltpu.VMEM((frames + 2 * HALF, width), BF16),
        pltpu.VMEM((frames, width), F32),
        pltpu.VMEM((frames, width), BF16),
        pltpu.VMEM((frames, width), BF16),
        pltpu.VMEM((2, RIM, width), BF16),
        pltpu.VMEM((2, RIM, width), BF16),
        pltpu.VMEM((2, RIM, width), BF16),
        pltpu.VMEM((chunks, frames + 2 * RIM, HDIM), F32),
        pltpu.VMEM((chunks, frames + 2 * HALF, HDIM), F32),
        pltpu.VMEM((4, frames, width), BF16),
        pltpu.VMEM((frames, width), BF16),
        pltpu.VMEM((frames, width), BF16),
        pltpu.VMEM((frames, width), BF16),
        pltpu.VMEM((frames, width), BF16),
        pltpu.VMEM((frames, width), F32),
        pltpu.VMEM((frames, width), F32),
        dma((3 * heads + 4,)),
        dma((5,)),
        dma((4, 2, heads)), dma((4, 2, heads)),
        dma((4,)), dma((4,)),
        dma((4,)), dma((4,)),
        dma((4, heads)), dma((4, heads)),
        dma((4,)), dma((4,)),
        dma((2,)), dma((2,)),
        dma((2,)), dma((2,)),
        dma((heads,)), dma((heads,)),
        dma((chunks,)), dma((chunks,)),
        dma((4, chunks)), dma((4, chunks)),
        dma((3, chunks)), dma((3, chunks)),
    ]
    shape = jax.ShapeDtypeStruct((frames, width), BF16)
    results = pl.pallas_call(
        functools.partial(kernel_body, count, heads),
        out_shape=(shape,) * 5,
        in_specs=[pl.BlockSpec(memory_space=pl.ANY)] * 7,
        out_specs=(pl.BlockSpec(memory_space=pl.ANY),) * 5,
        scratch_shapes=scratch,
        compiler_params=pltpu.CompilerParams(
            collective_id=0, has_side_effects=True, vmem_limit_bytes=56 * 1024 * 1024
        ),
        name="conformer",
    )(query_rows, key_rows, value_rows, inputs, out_weight, kernel, cotangent)
    return pl.pallas_call(
        copy_out,
        out_shape=(shape,) * 5,
        in_specs=[pl.BlockSpec(memory_space=pl.ANY)] * 5,
        out_specs=(pl.BlockSpec(memory_space=pl.ANY),) * 5,
        scratch_shapes=[pltpu.VMEM((5, frames, width), BF16), dma((2, 5))],
        compiler_params=pltpu.CompilerParams(vmem_limit_bytes=56 * 1024 * 1024),
        name="copy_out",
    )(*results)


def solution(mesh):
    placed = (
        P("ctx", "mp"),
        P("ctx", "mp"),
        P("ctx", "mp"),
        P("ctx", "mp"),
        P("mp", None),
        P(None, "mp"),
        P("ctx", "mp"),
    )
    return jax.shard_map(
        per_device,
        mesh=mesh,
        in_specs=placed,
        out_specs=(P("ctx", "mp"),) * 5,
        check_vma=False,
    )
```

```python
import functools
import math

import jax
import jax.numpy as jnp
from jax import lax
from jax.experimental import pallas as pl
from jax.experimental.pallas import tpu as pltpu
from jax.sharding import PartitionSpec as P

HDIM = 128
LOOK = 2
BLOCKS = 2 * LOOK + 1
RIM = 32
HALF = 16
MESH = pl.DeviceIdType.MESH
F32 = jnp.float32
BF16 = jnp.bfloat16


def nt(a, b):
    return lax.dot_general(a, b, (((1,), (1,)), ((), ())), preferred_element_type=F32)


def nn(a, b):
    return jnp.dot(a, b, preferred_element_type=F32)


def kernel_body(
    count,
    heads,
    q_hbm,
    k_hbm,
    v_hbm,
    in_hbm,
    w_hbm,
    tap_hbm,
    cot_hbm,
    out_hbm,
    gi_hbm,
    gq_hbm,
    gk_hbm,
    gv_hbm,
    qwin,
    kwin,
    vwin,
    dowin,
    lsewin,
    deltawin,
    probs,
    probs_t,
    att,
    w_own,
    w_sib,
    taps,
    inp,
    cotp,
    own_sum,
    part_send,
    part_recv,
    rim_send,
    rim_own,
    hpad,
    gpad,
    gfull,
    out_v,
    gq_v,
    gk_v,
    gv_v,
    gk_sum,
    gv_sum,
    local_sem,
    out_sem,
    kv_send,
    kv_recv,
    q_send,
    q_recv,
    lse_send,
    lse_recv,
    do_send,
    do_recv,
    delta_send,
    delta_recv,
    w_send,
    w_recv,
    cot_send,
    cot_recv,
    att_send,
    att_recv,
    part_ssem,
    part_rsem,
    rim_ssem,
    rim_rsem,
    gi_send,
    gi_recv,
):
    frames, width = inp.shape
    ntaps = taps.shape[0]
    scale = 1.0 / math.sqrt(HDIM)
    c = lax.axis_index("ctx")
    m = lax.axis_index("mp")
    right = lax.rem(c + 1, count)
    right2 = lax.rem(c + 2, count)
    left = lax.rem(c + count - 1, count)
    left2 = lax.rem(c + count - 2, count)
    sib_m = m + 1 - 2 * lax.rem(m, 2)
    far_m = lax.rem(m + 2, 4)
    far_sib_m = lax.rem(sib_m + 2, 4)
    sib = (c, sib_m)
    far = (c, far_m)

    barrier = pltpu.get_barrier_semaphore()
    exists = [c < count - 1, c > 0, c < count - 2, c > 1]
    targets = [right, left, right2, left2]
    places = [1, 3, 0, 4]

    def toward(i, plane=None):
        other = sib_m if plane is None else plane
        own = m if plane is None else plane
        return (jnp.where(exists[i], targets[i], c), jnp.where(exists[i], own, other))

    def turned(i, value, mirrored):
        return jnp.where(exists[i], value, mirrored)

    def place(i, slot):
        return pl.ds(pl.multiple_of(turned(i, slot, 4 - slot) * frames, frames), frames)

    partners = [toward(i) for i in range(4)] + [sib, far]
    for device in partners:
        pl.semaphore_signal(barrier, inc=1, device_id=device, device_id_type=MESH)

    def local(src, dst, at):
        copy = pltpu.make_async_copy(src, dst, local_sem.at[at])
        copy.start()
        return copy

    def remote(src, dst, send, recv, device):
        return pltpu.make_async_remote_copy(
            src_ref=src, dst_ref=dst, send_sem=send, recv_sem=recv,
            device_id=device, device_id_type=MESH,
        )

    class Crossing:
        def __init__(self, sent, due):
            self.start, self.wait_send, self.wait_recv = sent.start, sent.wait_send, due.wait_recv

    def shift(src, dst, due_dst, send, recv, due_recv, device):
        return Crossing(
            remote(src, dst, send, recv, device), remote(src, due_dst, send, due_recv, device)
        )

    def cols(index):
        return slice(index * HDIM, (index + 1) * HDIM)

    def block(slot):
        return slice(slot * frames, (slot + 1) * frames)

    def wide(index):
        return pl.ds(pl.multiple_of(index * width, width), width)

    mid = block(LOOK)
    loads = {}
    for h in range(heads):
        loads["q", h] = local(q_hbm.at[:, cols(h)], qwin.at[h, mid], h)
        loads["k", h] = local(k_hbm.at[:, cols(h)], kwin.at[h, mid], heads + h)
        loads["v", h] = local(v_hbm.at[:, cols(h)], vwin.at[h, mid], 2 * heads + h)
    at = 3 * heads
    loads["w"] = local(w_hbm, w_own, at)
    loads["taps"] = local(tap_hbm, taps, at + 1)
    loads["inp"] = local(in_hbm, inp, at + 2)
    loads["cot"] = local(cot_hbm, cotp.at[HALF : HALF + frames], at + 3)

    pl.semaphore_wait(barrier, len(partners))

    first = {}
    second = {}
    for h in range(heads):
        for i, (src, win) in enumerate(((k_hbm, kwin), (v_hbm, vwin))):
            for side in range(2):
                near_slot, far_slot = places[side], places[2 + side]
                first[h, i, side] = shift(
                    src.at[:, cols(h)], win.at[h, place(side, near_slot)], win.at[h, block(near_slot)],
                    kv_send.at[side, i, h], kv_recv.at[turned(side, side, 1 - side), i, h],
                    kv_recv.at[side, i, h], toward(side),
                )
                first[h, i, side].start()
                second[h, i, side] = shift(
                    win.at[h, block(near_slot)], win.at[h, place(side, far_slot)], win.at[h, block(far_slot)],
                    kv_send.at[2 + side, i, h], kv_recv.at[2 + turned(side, side, 1 - side), i, h],
                    kv_recv.at[2 + side, i, h], toward(side),
                )

    early = [
        remote(w_hbm.at[:, wide(sib_m)], w_sib.at[0], w_send.at[0], w_recv.at[0], sib),
        remote(w_hbm.at[:, wide(far_sib_m)], w_sib.at[1], w_send.at[1], w_recv.at[1], sib),
    ]
    cot_starts = (0, HALF + frames)
    for side, rows in enumerate((slice(frames - HALF, frames), slice(0, HALF))):
        start = turned(side, cot_starts[side], cot_starts[1 - side])
        early.append(shift(
            cot_hbm.at[rows], cotp.at[pl.ds(pl.multiple_of(start, HALF), HALF)],
            cotp.at[cot_starts[side] : cot_starts[side] + HALF],
            cot_send.at[side], cot_recv.at[turned(side, side, 1 - side)], cot_recv.at[side], toward(side),
        ))
    for h in range(heads):
        for side in range(2):
            for i in range(2):
                first[h, i, side].wait_recv()
                second[h, i, side].start()

    for copy in early:
        copy.start()

    owner = lax.shift_right_logical(
        lax.broadcasted_iota(jnp.int32, (1, BLOCKS * frames), 1), 7
    ) + c
    valid = (owner >= LOOK) & (owner < count + LOOK)
    lane = lax.broadcasted_iota(jnp.int32, (frames, HDIM), 1)

    def spread_to(i, win, send, recv, source=mid):
        return shift(
            win.at[:, source], win.at[:, place(i, places[i])], win.at[:, block(places[i])],
            send.at[i], recv.at[turned(i, i, i ^ 1)], recv.at[i], toward(i),
        )

    def relay_to(side, win, send, recv):
        near_slot, far_slot = places[side], places[2 + side]
        return shift(
            win.at[:, block(near_slot)], win.at[:, place(side, far_slot)], win.at[:, block(far_slot)],
            send.at[2 + side], recv.at[2 + turned(side, side, 1 - side)], recv.at[2 + side], toward(side),
        )

    queries = [spread_to(side, qwin, q_send, q_recv) for side in range(2)]
    queries += [relay_to(side, qwin, q_send, q_recv) for side in range(2)]

    stat = jnp.zeros((frames, HDIM), F32)
    shares = []
    for h in range(heads):
        loads["q", h].wait()
        loads["k", h].wait()
        loads["v", h].wait()
        for side in range(2):
            for i in range(2):
                second[h, i, side].wait_recv()
        if h == heads - 1:
            queries[0].start()
            queries[1].start()
        scores = nt(qwin[h, mid], kwin[h]) * scale
        scores = jnp.where(valid, scores, -jnp.inf)
        top = jnp.max(scores, axis=1, keepdims=True)
        weights = jnp.exp(scores - top)
        total = jnp.sum(weights, axis=1, keepdims=True)
        stat = jnp.where(lane == h, top + jnp.log(total), stat)
        prob = weights * (1.0 / total)
        probs[h] = prob
        att[0, :, cols(h)] = nn(prob.astype(BF16), vwin[h]).astype(BF16)
        share = remote(att.at[0, :, cols(h)], att.at[1, :, cols(h)], att_send.at[h], att_recv.at[h], sib)
        share.start()
        shares.append(share)
    lsewin[:, mid] = jnp.transpose(stat)[0:8]

    loads["w"].wait()
    early[0].wait_recv()
    early[1].wait_recv()
    for share in shares:
        share.wait_recv()
    parts = []
    for j in range(width // HDIM):
        lanes = cols(j)
        far_cols = pl.ds(pl.multiple_of(far_m * width + j * HDIM, HDIM), HDIM)
        part_send[:, lanes] = (nn(att[0], w_own[:, far_cols]) + nn(att[1], w_sib[1, :, lanes])).astype(BF16)
        group = [
            remote(part_send.at[:, lanes], part_recv.at[:, lanes], part_ssem.at[j], part_rsem.at[j], far)
        ]
        for copy in group:
            copy.start()
        parts.append(group)
    loads["inp"].wait()
    own_part = nn(att[0], w_own[:, wide(m)])
    summed = own_part + nn(att[1], w_sib[0]) + inp[...].astype(F32)
    own_sum[...] = summed

    totals = [spread_to(i, lsewin, lse_send, lse_recv) for i in range(4)]
    for copy in totals:
        copy.start()

    loads["taps"].wait()
    loads["cot"].wait()
    early[2].wait_recv()
    early[3].wait_recv()

    row = lax.broadcasted_iota(jnp.int32, (frames + 2 * HALF, HDIM), 0)
    inside = ((row >= HALF) | (c > 0)) & ((row < HALF + frames) | (c < count - 1))
    for j in range(width // HDIM):
        lanes = cols(j)
        for copy in parts[j]:
            copy.wait_recv()
        hidden = (own_sum[:, lanes] + part_recv[:, lanes].astype(F32)).astype(BF16)
        hpad[j, RIM : RIM + frames] = hidden.astype(F32)
        rim_send[0, :, lanes] = hidden[frames - RIM : frames]
        rim_send[1, :, lanes] = hidden[0:RIM]
    rims = []
    for side in range(2):
        turn = turned(side, side, 1 - side)
        rims.append(shift(
            rim_send.at[side], rim_own.at[turn], rim_own.at[side],
            rim_ssem.at[side], rim_rsem.at[turn], rim_rsem.at[side], toward(side),
        ))
        rims[-1].start()

    def conv_rows(j, start, rows):
        lanes = cols(j)
        conv = jnp.zeros((rows, HDIM), F32)
        for tap in range(ntaps):
            at = start + RIM - HALF + 1 + tap
            conv = conv + taps[tap : tap + 1, lanes] * hpad[j, at : at + rows]
        gate = jax.nn.sigmoid(conv)
        swish = conv * gate
        low, high = max(start, 0), min(start + rows, frames)
        out_v[low:high, lanes] = (
            hpad[j, RIM + low : RIM + high] + swish[low - start : high - start]
        ).astype(BF16)
        span = slice(start + HALF, start + HALF + rows)
        cot = cotp[span, lanes].astype(F32)
        grad_conv = (cot * (gate + swish * (1.0 - gate))).astype(BF16).astype(F32)
        gpad[j, span] = jnp.where(inside[span], grad_conv, 0.0)

    def grad_rows(j, start, rows):
        lanes = cols(j)
        grad = cotp[HALF + start : HALF + start + rows, lanes].astype(F32)
        for tap in range(ntaps):
            at = start + 2 * HALF - 1 - tap
            grad = grad + taps[tap : tap + 1, lanes] * gpad[j, at : at + rows]
        gfull[0, start : start + rows, lanes] = grad.astype(BF16)

    edges = ((0, RIM), (frames - RIM, RIM))
    spans = (((RIM, frames - 2 * RIM),), edges)
    spread = []

    def leave(part, start, rows, lanes):
        at, n = slice(start, start + rows), len(spread)
        pieces = (
            remote(gfull.at[0, at, lanes], gfull.at[1, at, lanes], gi_send.at[0, n], gi_recv.at[0, n], sib),
            remote(gfull.at[0, at, lanes], gfull.at[2, at, lanes], gi_send.at[1, n], gi_recv.at[1, n], far),
            remote(gfull.at[2, at, lanes], gfull.at[3, at, lanes], gi_send.at[2, n], gi_recv.at[2, n], sib),
        )
        pieces[1].start()
        pieces[0].start()
        spread.append((part,) + pieces)

    for j in range(width // HDIM):
        conv_rows(j, HALF, frames - 2 * HALF)
        grad_rows(j, RIM, frames - 2 * RIM)
        if j % 2 == 1:
            leave(0, RIM, frames - 2 * RIM, slice((j - 1) * HDIM, (j + 1) * HDIM))
    for copy in rims:
        copy.wait_recv()
    for j in range(width // HDIM):
        lanes = cols(j)
        hpad[j, 0:RIM] = jnp.where(c > 0, rim_own[0, :, lanes].astype(F32), 0.0)
        hpad[j, RIM + frames : 2 * RIM + frames] = jnp.where(c < count - 1, rim_own[1, :, lanes].astype(F32), 0.0)
        conv_rows(j, -HALF, 2 * HALF)
        conv_rows(j, frames - HALF, 2 * HALF)
        for start, rows in edges:
            grad_rows(j, start, rows)
    for start, rows in edges:
        leave(1, start, rows, slice(0, width))

    stores = [
        pltpu.make_async_copy(out_v, out_hbm, out_sem.at[0]),
        pltpu.make_async_copy(gfull.at[0], gi_hbm, out_sem.at[1]),
    ]
    for copy in stores:
        copy.start()

    for side in range(2):
        queries[side].wait_recv()
        queries[2 + side].start()

    own_up = nt(gfull[0], w_own[:, wide(m)])
    for _, to_sib, _, _ in spread:
        to_sib.wait_recv()
    own_up = own_up + nt(gfull[1], w_own[:, wide(sib_m)])
    ups = []
    second_ups = []
    def rows_of(take, part):
        pieces = [take(slice(start, start + rows)) for start, rows in spans[part]]
        return pieces[0] if len(pieces) == 1 else jnp.concatenate(pieces, axis=0)

    for r in range(2):
        mine = [piece for piece in spread if piece[0] == r]
        for _, _, to_far, relay in mine:
            to_far.wait_recv()
            relay.start()
        up = rows_of(lambda at: own_up[at], r) + nt(rows_of(lambda at: gfull[2, at], r), w_own[:, wide(far_m)])
        for _, _, _, relay in mine:
            relay.wait_recv()
        up = up + nt(rows_of(lambda at: gfull[3, at], r), w_own[:, wide(far_sib_m)])
        upstream = up.astype(BF16)
        begun = 0
        for start, rows in spans[r]:
            for h in range(heads):
                dowin[h, LOOK * frames + start : LOOK * frames + start + rows] = upstream[begun : begun + rows, cols(h)]
            begun += rows

        for start, rows in spans[r]:
            n = len(ups) // 2

            def rows_at(slot, start=start, rows=rows):
                return pl.ds(pl.multiple_of(slot * frames + start, RIM), rows)

            for side in range(2):
                turn = turned(side, side, 1 - side)
                near_slot, far_slot = places[side], places[2 + side]
                own_at, near_at, far_at = rows_at(LOOK), rows_at(near_slot), rows_at(far_slot)
                near_to = rows_at(turned(side, near_slot, 4 - near_slot))
                far_to = rows_at(turned(side, far_slot, 4 - far_slot))
                ups.append(shift(
                    dowin.at[:, own_at], dowin.at[:, near_to], dowin.at[:, near_at],
                    do_send.at[side, n], do_recv.at[turn, n], do_recv.at[side, n], toward(side),
                ))
                ups[-1].start()
                second_ups.append(shift(
                    dowin.at[:, near_at], dowin.at[:, far_to], dowin.at[:, far_at],
                    do_send.at[2 + side, n], do_recv.at[2 + turn, n], do_recv.at[2 + side, n], toward(side),
                ))

    delta = []
    stat = jnp.zeros((frames, HDIM), F32)
    for h in range(heads):
        delta.append(
            jnp.sum(dowin[h, mid].astype(F32) * att[0, :, cols(h)].astype(F32), axis=1, keepdims=True)
        )
        stat = jnp.where(lane == h, delta[h], stat)
    deltawin[:, mid] = jnp.transpose(stat)[0:8]
    deltas = [spread_to(i, deltawin, delta_send, delta_recv) for i in range(4)]
    for copy in deltas:
        copy.start()

    def query_grad(h):
        dots = nt(dowin[h, mid], vwin[h])
        grad_scores = (probs[h] * (dots - delta[h]) * scale).astype(BF16)
        gq_v[:, cols(h)] = nn(grad_scores, kwin[h]).astype(BF16)

    def key_grad(h, span):
        prob_t = probs_t[h, :, span]
        d_value = nn(prob_t.astype(BF16), dowin[h, span])
        dots_t = nt(vwin[h, mid], dowin[h, span])
        grad_t = (prob_t * (dots_t - deltawin[h : h + 1, span]) * scale).astype(BF16)
        return nn(grad_t, qwin[h, span]), d_value

    for h in range(heads):
        query_grad(h)
    stores.append(pltpu.make_async_copy(gq_v, gq_hbm, out_sem.at[2]))
    stores[-1].start()
    for one, two in zip(ups, second_ups):
        one.wait_recv()
        two.start()
    for copy in deltas:
        copy.wait_recv()

    for copy in queries[2:] + totals:
        copy.wait_recv()
    for h in range(heads):
        scores_t = nt(kwin[h, mid], qwin[h]) * scale
        probs_t[h] = jnp.where(valid, jnp.exp(scores_t - lsewin[h : h + 1]), 0.0)
    near = slice(frames, 4 * frames)
    for h in range(heads):
        gk_sum[:, cols(h)], gv_sum[:, cols(h)] = key_grad(h, near)
    for copy in second_ups:
        copy.wait_recv()
    for h in range(heads):
        low_k, low_v = key_grad(h, block(0))
        high_k, high_v = key_grad(h, block(4))
        gk_v[:, cols(h)] = (gk_sum[:, cols(h)] + low_k + high_k).astype(BF16)
        gv_v[:, cols(h)] = (gv_sum[:, cols(h)] + low_v + high_v).astype(BF16)
    stores.append(pltpu.make_async_copy(gk_v, gk_hbm, out_sem.at[3]))
    stores[-1].start()
    stores.append(pltpu.make_async_copy(gv_v, gv_hbm, out_sem.at[4]))
    stores[-1].start()

    for copy in list(first.values()) + list(second.values()) + early + shares + queries + totals:
        copy.wait_send()
    for copy in ups + second_ups + deltas:
        copy.wait_send()
    for group in parts + [rims] + [piece[1:] for piece in spread]:
        for copy in group:
            copy.wait_send()
    for copy in stores:
        copy.wait()


def copy_out(*refs):
    sources, targets, held, sems = refs[:5], refs[5:10], refs[10], refs[11]
    taken = [pltpu.make_async_copy(source, held.at[i], sems.at[0, i]) for i, source in enumerate(sources)]
    given = [pltpu.make_async_copy(held.at[i], target, sems.at[1, i]) for i, target in enumerate(targets)]
    for copy in taken:
        copy.start()
    for one, two in zip(taken, given):
        one.wait()
        two.start()
    for copy in given:
        copy.wait()


def per_device(query_rows, key_rows, value_rows, inputs, out_weight, kernel, cotangent):
    frames, width = query_rows.shape
    heads = width // HDIM
    count = lax.axis_size("ctx")
    window = BLOCKS * frames
    full = out_weight.shape[1]
    chunks = width // HDIM
    taps = kernel.shape[0]
    dma = pltpu.SemaphoreType.DMA
    win = pltpu.VMEM((heads, window, HDIM), BF16)
    scratch = [
        win, win, win, win,
        pltpu.VMEM((8, window), F32),
        pltpu.VMEM((8, window), F32),
        pltpu.VMEM((heads, frames, window), F32),
        pltpu.VMEM((heads, frames, window), F32),
        pltpu.VMEM((2, frames, width), BF16),
        pltpu.VMEM((width, full), BF16),
        pltpu.VMEM((2, width, width), BF16),
        pltpu.VMEM((taps, width), F32),
        pltpu.VMEM((frames, width), BF16),
        pltpu.VMEM((frames + 2 * HALF, width), BF16),
        pltpu.VMEM((frames, width), F32),
        pltpu.VMEM((frames, width), BF16),
        pltpu.VMEM((frames, width), BF16),
        pltpu.VMEM((2, RIM, width), BF16),
        pltpu.VMEM((2, RIM, width), BF16),
        pltpu.VMEM((chunks, frames + 2 * RIM, HDIM), F32),
        pltpu.VMEM((chunks, frames + 2 * HALF, HDIM), F32),
        pltpu.VMEM((4, frames, width), BF16),
        pltpu.VMEM((frames, width), BF16),
        pltpu.VMEM((frames, width), BF16),
        pltpu.VMEM((frames, width), BF16),
        pltpu.VMEM((frames, width), BF16),
        pltpu.VMEM((frames, width), F32),
        pltpu.VMEM((frames, width), F32),
        dma((3 * heads + 4,)),
        dma((5,)),
        dma((4, 2, heads)), dma((4, 2, heads)),
        dma((4,)), dma((4,)),
        dma((4,)), dma((4,)),
        dma((4, heads)), dma((4, heads)),
        dma((4,)), dma((4,)),
        dma((2,)), dma((2,)),
        dma((2,)), dma((2,)),
        dma((heads,)), dma((heads,)),
        dma((chunks,)), dma((chunks,)),
        dma((2,)), dma((2,)),
        dma((3, 4)), dma((3, 4)),
    ]
    shape = jax.ShapeDtypeStruct((frames, width), BF16)
    results = pl.pallas_call(
        functools.partial(kernel_body, count, heads),
        out_shape=(shape,) * 5,
        in_specs=[pl.BlockSpec(memory_space=pl.ANY)] * 7,
        out_specs=(pl.BlockSpec(memory_space=pl.ANY),) * 5,
        scratch_shapes=scratch,
        compiler_params=pltpu.CompilerParams(
            collective_id=0, has_side_effects=True, vmem_limit_bytes=56 * 1024 * 1024
        ),
        name="conformer",
    )(query_rows, key_rows, value_rows, inputs, out_weight, kernel, cotangent)
    return pl.pallas_call(
        copy_out,
        out_shape=(shape,) * 5,
        in_specs=[pl.BlockSpec(memory_space=pl.ANY)] * 5,
        out_specs=(pl.BlockSpec(memory_space=pl.ANY),) * 5,
        scratch_shapes=[pltpu.VMEM((5, frames, width), BF16), dma((2, 5))],
        compiler_params=pltpu.CompilerParams(vmem_limit_bytes=56 * 1024 * 1024),
        name="copy_out",
    )(*results)


def solution(mesh):
    placed = (
        P("ctx", "mp"),
        P("ctx", "mp"),
        P("ctx", "mp"),
        P("ctx", "mp"),
        P("mp", None),
        P(None, "mp"),
        P("ctx", "mp"),
    )
    return jax.shard_map(
        per_device,
        mesh=mesh,
        in_specs=placed,
        out_specs=(P("ctx", "mp"),) * 5,
        check_vma=False,
    )
```

```python
import functools
import math

import jax
import jax.numpy as jnp
from jax import lax
from jax.experimental import pallas as pl
from jax.experimental.pallas import tpu as pltpu
from jax.sharding import PartitionSpec as P

HDIM = 128
LOOK = 2
BLOCKS = 2 * LOOK + 1
RIM = 32
HALF = 16
MESH = pl.DeviceIdType.MESH
F32 = jnp.float32
BF16 = jnp.bfloat16


def nt(a, b):
    return lax.dot_general(a, b, (((1,), (1,)), ((), ())), preferred_element_type=F32)


def nn(a, b):
    return jnp.dot(a, b, preferred_element_type=F32)


def kernel_body(
    count,
    heads,
    q_hbm,
    k_hbm,
    v_hbm,
    in_hbm,
    w_hbm,
    tap_hbm,
    cot_hbm,
    out_hbm,
    gi_hbm,
    gq_hbm,
    gk_hbm,
    gv_hbm,
    qwin,
    kwin,
    vwin,
    dowin,
    lsewin,
    deltawin,
    probs,
    probs_t,
    att,
    w_own,
    w_sib,
    taps,
    inp,
    cotp,
    own_sum,
    part_send,
    part_recv,
    rim_send,
    rim_own,
    hpad,
    gpad,
    gfull,
    out_v,
    gq_v,
    gk_v,
    gv_v,
    gk_sum,
    gv_sum,
    local_sem,
    out_sem,
    kv_send,
    kv_recv,
    q_send,
    q_recv,
    lse_send,
    lse_recv,
    do_send,
    do_recv,
    delta_send,
    delta_recv,
    w_send,
    w_recv,
    cot_send,
    cot_recv,
    att_send,
    att_recv,
    part_ssem,
    part_rsem,
    rim_ssem,
    rim_rsem,
    gi_send,
    gi_recv,
):
    frames, width = inp.shape
    ntaps = taps.shape[0]
    scale = 1.0 / math.sqrt(HDIM)
    c = lax.axis_index("ctx")
    m = lax.axis_index("mp")
    right = lax.rem(c + 1, count)
    right2 = lax.rem(c + 2, count)
    left = lax.rem(c + count - 1, count)
    left2 = lax.rem(c + count - 2, count)
    sib_m = m + 1 - 2 * lax.rem(m, 2)
    far_m = lax.rem(m + 2, 4)
    far_sib_m = lax.rem(sib_m + 2, 4)
    sib = (c, sib_m)
    far = (c, far_m)

    barrier = pltpu.get_barrier_semaphore()
    exists = [c < count - 1, c > 0, c < count - 2, c > 1]
    targets = [right, left, right2, left2]
    places = [1, 3, 0, 4]

    def toward(i, plane=None):
        other = sib_m if plane is None else plane
        own = m if plane is None else plane
        return (jnp.where(exists[i], targets[i], c), jnp.where(exists[i], own, other))

    def turned(i, value, mirrored):
        return jnp.where(exists[i], value, mirrored)

    def place(i, slot):
        return pl.ds(pl.multiple_of(turned(i, slot, 4 - slot) * frames, frames), frames)

    partners = [toward(i) for i in range(4)] + [sib, far]
    for device in partners:
        pl.semaphore_signal(barrier, inc=1, device_id=device, device_id_type=MESH)

    def local(src, dst, at):
        copy = pltpu.make_async_copy(src, dst, local_sem.at[at])
        copy.start()
        return copy

    def remote(src, dst, send, recv, device):
        return pltpu.make_async_remote_copy(
            src_ref=src, dst_ref=dst, send_sem=send, recv_sem=recv,
            device_id=device, device_id_type=MESH,
        )

    class Crossing:
        def __init__(self, sent, due):
            self.start, self.wait_send, self.wait_recv = sent.start, sent.wait_send, due.wait_recv

    def shift(src, dst, due_dst, send, recv, due_recv, device):
        return Crossing(
            remote(src, dst, send, recv, device), remote(src, due_dst, send, due_recv, device)
        )

    def cols(index):
        return slice(index * HDIM, (index + 1) * HDIM)

    def block(slot):
        return slice(slot * frames, (slot + 1) * frames)

    def wide(index):
        return pl.ds(pl.multiple_of(index * width, width), width)

    mid = block(LOOK)
    pl.semaphore_wait(barrier, len(partners))

    first = {}
    second = {}
    for h in range(heads):
        for i, (src, win) in enumerate(((k_hbm, kwin), (v_hbm, vwin))):
            for side in range(2):
                near_slot, far_slot = places[side], places[2 + side]
                first[h, i, side] = shift(
                    src.at[:, cols(h)], win.at[h, place(side, near_slot)], win.at[h, block(near_slot)],
                    kv_send.at[side, i, h], kv_recv.at[turned(side, side, 1 - side), i, h],
                    kv_recv.at[side, i, h], toward(side),
                )
                first[h, i, side].start()
                second[h, i, side] = shift(
                    win.at[h, block(near_slot)], win.at[h, place(side, far_slot)], win.at[h, block(far_slot)],
                    kv_send.at[2 + side, i, h], kv_recv.at[2 + turned(side, side, 1 - side), i, h],
                    kv_recv.at[2 + side, i, h], toward(side),
                )

    early = [
        remote(w_hbm.at[:, wide(sib_m)], w_sib.at[0], w_send.at[0], w_recv.at[0], sib),
        remote(w_hbm.at[:, wide(far_sib_m)], w_sib.at[1], w_send.at[1], w_recv.at[1], sib),
    ]
    cot_starts = (0, HALF + frames)
    for side, rows in enumerate((slice(frames - HALF, frames), slice(0, HALF))):
        start = turned(side, cot_starts[side], cot_starts[1 - side])
        early.append(shift(
            cot_hbm.at[rows], cotp.at[pl.ds(pl.multiple_of(start, HALF), HALF)],
            cotp.at[cot_starts[side] : cot_starts[side] + HALF],
            cot_send.at[side], cot_recv.at[turned(side, side, 1 - side)], cot_recv.at[side], toward(side),
        ))
    loads = {}
    for h in range(heads):
        loads["q", h] = local(q_hbm.at[:, cols(h)], qwin.at[h, mid], h)
        loads["k", h] = local(k_hbm.at[:, cols(h)], kwin.at[h, mid], heads + h)
        loads["v", h] = local(v_hbm.at[:, cols(h)], vwin.at[h, mid], 2 * heads + h)
    at = 3 * heads
    loads["w"] = local(w_hbm, w_own, at)
    loads["taps"] = local(tap_hbm, taps, at + 1)
    loads["inp"] = local(in_hbm, inp, at + 2)
    loads["cot"] = local(cot_hbm, cotp.at[HALF : HALF + frames], at + 3)

    for h in range(heads):
        for side in range(2):
            for i in range(2):
                first[h, i, side].wait_recv()
                second[h, i, side].start()

    for copy in early:
        copy.start()

    owner = lax.shift_right_logical(
        lax.broadcasted_iota(jnp.int32, (1, BLOCKS * frames), 1), 7
    ) + c
    valid = (owner >= LOOK) & (owner < count + LOOK)
    lane = lax.broadcasted_iota(jnp.int32, (frames, HDIM), 1)

    def spread_to(i, win, send, recv, source=mid):
        return shift(
            win.at[:, source], win.at[:, place(i, places[i])], win.at[:, block(places[i])],
            send.at[i], recv.at[turned(i, i, i ^ 1)], recv.at[i], toward(i),
        )

    def relay_to(side, win, send, recv):
        near_slot, far_slot = places[side], places[2 + side]
        return shift(
            win.at[:, block(near_slot)], win.at[:, place(side, far_slot)], win.at[:, block(far_slot)],
            send.at[2 + side], recv.at[2 + turned(side, side, 1 - side)], recv.at[2 + side], toward(side),
        )

    queries = [spread_to(side, qwin, q_send, q_recv) for side in range(2)]
    queries += [relay_to(side, qwin, q_send, q_recv) for side in range(2)]

    stat = jnp.zeros((frames, HDIM), F32)
    shares = []
    for h in range(heads):
        loads["q", h].wait()
        loads["k", h].wait()
        loads["v", h].wait()
        for side in range(2):
            for i in range(2):
                second[h, i, side].wait_recv()
        if h == heads - 1:
            queries[0].start()
            queries[1].start()
        scores = nt(qwin[h, mid], kwin[h]) * scale
        scores = jnp.where(valid, scores, -jnp.inf)
        top = jnp.max(scores, axis=1, keepdims=True)
        weights = jnp.exp(scores - top)
        total = jnp.sum(weights, axis=1, keepdims=True)
        stat = jnp.where(lane == h, top + jnp.log(total), stat)
        prob = weights * (1.0 / total)
        probs[h] = prob
        att[0, :, cols(h)] = nn(prob.astype(BF16), vwin[h]).astype(BF16)
        share = remote(att.at[0, :, cols(h)], att.at[1, :, cols(h)], att_send.at[h], att_recv.at[h], sib)
        share.start()
        shares.append(share)

    loads["w"].wait()
    far_part = nn(att[0], w_own[:, wide(far_m)])
    lsewin[:, mid] = jnp.transpose(stat)[0:8]
    early[0].wait_recv()
    early[1].wait_recv()
    for share in shares:
        share.wait_recv()
    parts = []
    for j in range(width // HDIM):
        lanes = cols(j)
        part_send[:, lanes] = (far_part[:, lanes] + nn(att[1], w_sib[1, :, lanes])).astype(BF16)
        group = [
            remote(part_send.at[:, lanes], part_recv.at[:, lanes], part_ssem.at[j], part_rsem.at[j], far)
        ]
        for copy in group:
            copy.start()
        parts.append(group)
    loads["inp"].wait()
    own_part = nn(att[0], w_own[:, wide(m)])
    summed = own_part + nn(att[1], w_sib[0]) + inp[...].astype(F32)
    own_sum[...] = summed

    totals = [spread_to(i, lsewin, lse_send, lse_recv) for i in range(4)]
    for copy in totals:
        copy.start()

    loads["taps"].wait()
    loads["cot"].wait()
    early[2].wait_recv()
    early[3].wait_recv()

    row = lax.broadcasted_iota(jnp.int32, (frames + 2 * HALF, HDIM), 0)
    inside = ((row >= HALF) | (c > 0)) & ((row < HALF + frames) | (c < count - 1))
    for j in range(width // HDIM):
        lanes = cols(j)
        for copy in parts[j]:
            copy.wait_recv()
        hidden = (own_sum[:, lanes] + part_recv[:, lanes].astype(F32)).astype(BF16)
        hpad[j, RIM : RIM + frames] = hidden.astype(F32)
        rim_send[0, :, lanes] = hidden[frames - RIM : frames]
        rim_send[1, :, lanes] = hidden[0:RIM]
    rims = []
    for side in range(2):
        turn = turned(side, side, 1 - side)
        rims.append(shift(
            rim_send.at[side], rim_own.at[turn], rim_own.at[side],
            rim_ssem.at[side], rim_rsem.at[turn], rim_rsem.at[side], toward(side),
        ))
        rims[-1].start()

    def conv_rows(j, start, rows):
        lanes = cols(j)
        conv = jnp.zeros((rows, HDIM), F32)
        for tap in range(ntaps):
            at = start + RIM - HALF + 1 + tap
            conv = conv + taps[tap : tap + 1, lanes] * hpad[j, at : at + rows]
        gate = jax.nn.sigmoid(conv)
        swish = conv * gate
        low, high = max(start, 0), min(start + rows, frames)
        out_v[low:high, lanes] = (
            hpad[j, RIM + low : RIM + high] + swish[low - start : high - start]
        ).astype(BF16)
        span = slice(start + HALF, start + HALF + rows)
        cot = cotp[span, lanes].astype(F32)
        grad_conv = (cot * (gate + swish * (1.0 - gate))).astype(BF16).astype(F32)
        gpad[j, span] = jnp.where(inside[span], grad_conv, 0.0)

    def grad_rows(j, start, rows):
        lanes = cols(j)
        grad = cotp[HALF + start : HALF + start + rows, lanes].astype(F32)
        for tap in range(ntaps):
            at = start + 2 * HALF - 1 - tap
            grad = grad + taps[tap : tap + 1, lanes] * gpad[j, at : at + rows]
        gfull[0, start : start + rows, lanes] = grad.astype(BF16)

    edges = ((0, RIM), (frames - RIM, RIM))
    spans = (((RIM, frames - 2 * RIM),), edges)
    spread = []

    def leave(part, start, rows, lanes):
        at, n = slice(start, start + rows), len(spread)
        pieces = (
            remote(gfull.at[0, at, lanes], gfull.at[1, at, lanes], gi_send.at[0, n], gi_recv.at[0, n], sib),
            remote(gfull.at[0, at, lanes], gfull.at[2, at, lanes], gi_send.at[1, n], gi_recv.at[1, n], far),
            remote(gfull.at[2, at, lanes], gfull.at[3, at, lanes], gi_send.at[2, n], gi_recv.at[2, n], sib),
        )
        pieces[1].start()
        pieces[0].start()
        spread.append((part,) + pieces)

    for j in range(width // HDIM):
        conv_rows(j, HALF, frames - 2 * HALF)
        grad_rows(j, RIM, frames - 2 * RIM)
        if j % 2 == 1:
            leave(0, RIM, frames - 2 * RIM, slice((j - 1) * HDIM, (j + 1) * HDIM))
    for copy in rims:
        copy.wait_recv()
    for j in range(width // HDIM):
        lanes = cols(j)
        hpad[j, 0:RIM] = jnp.where(c > 0, rim_own[0, :, lanes].astype(F32), 0.0)
        hpad[j, RIM + frames : 2 * RIM + frames] = jnp.where(c < count - 1, rim_own[1, :, lanes].astype(F32), 0.0)
        conv_rows(j, -HALF, 2 * HALF)
        conv_rows(j, frames - HALF, 2 * HALF)
        for start, rows in edges:
            grad_rows(j, start, rows)
    for start, rows in edges:
        leave(1, start, rows, slice(0, width))

    stores = [
        pltpu.make_async_copy(out_v, out_hbm, out_sem.at[0]),
        pltpu.make_async_copy(gfull.at[0], gi_hbm, out_sem.at[1]),
    ]
    for copy in stores:
        copy.start()

    for side in range(2):
        queries[side].wait_recv()
        queries[2 + side].start()

    ups = []
    second_ups = []
    def rows_of(take, part):
        pieces = [take(slice(start, start + rows)) for start, rows in spans[part]]
        return pieces[0] if len(pieces) == 1 else jnp.concatenate(pieces, axis=0)

    for r in range(2):
        mine = [piece for piece in spread if piece[0] == r]
        up = nt(rows_of(lambda at: gfull[0, at], r), w_own[:, wide(m)])
        for _, to_sib, _, _ in mine:
            to_sib.wait_recv()
        up = up + nt(rows_of(lambda at: gfull[1, at], r), w_own[:, wide(sib_m)])
        for _, _, to_far, relay in mine:
            to_far.wait_recv()
            relay.start()
        up = up + nt(rows_of(lambda at: gfull[2, at], r), w_own[:, wide(far_m)])
        for _, _, _, relay in mine:
            relay.wait_recv()
        up = up + nt(rows_of(lambda at: gfull[3, at], r), w_own[:, wide(far_sib_m)])
        upstream = up.astype(BF16)
        begun = 0
        for start, rows in spans[r]:
            for h in range(heads):
                dowin[h, LOOK * frames + start : LOOK * frames + start + rows] = upstream[begun : begun + rows, cols(h)]
            begun += rows

        for start, rows in spans[r]:
            n = len(ups) // 2

            def rows_at(slot, start=start, rows=rows):
                return pl.ds(pl.multiple_of(slot * frames + start, RIM), rows)

            for side in range(2):
                turn = turned(side, side, 1 - side)
                near_slot, far_slot = places[side], places[2 + side]
                own_at, near_at, far_at = rows_at(LOOK), rows_at(near_slot), rows_at(far_slot)
                near_to = rows_at(turned(side, near_slot, 4 - near_slot))
                far_to = rows_at(turned(side, far_slot, 4 - far_slot))
                ups.append(shift(
                    dowin.at[:, own_at], dowin.at[:, near_to], dowin.at[:, near_at],
                    do_send.at[side, n], do_recv.at[turn, n], do_recv.at[side, n], toward(side),
                ))
                ups[-1].start()
                if r == 0:
                    second_ups.append(shift(
                        dowin.at[:, near_at], dowin.at[:, far_to], dowin.at[:, far_at],
                        do_send.at[2 + side, n], do_recv.at[2 + turn, n], do_recv.at[2 + side, n], toward(side),
                    ))
                    continue
                over = 2 + side
                far_to = rows_at(turned(over, far_slot, 4 - far_slot))
                second_ups.append(shift(
                    dowin.at[:, own_at], dowin.at[:, far_to], dowin.at[:, far_at],
                    do_send.at[over, n], do_recv.at[turned(over, over, over ^ 1), n], do_recv.at[over, n], toward(over),
                ))
                second_ups[-1].start()

    delta = []
    stat = jnp.zeros((frames, HDIM), F32)
    for h in range(heads):
        delta.append(
            jnp.sum(dowin[h, mid].astype(F32) * att[0, :, cols(h)].astype(F32), axis=1, keepdims=True)
        )
        stat = jnp.where(lane == h, delta[h], stat)
    deltawin[:, mid] = jnp.transpose(stat)[0:8]
    deltas = [spread_to(i, deltawin, delta_send, delta_recv) for i in range(4)]
    for copy in deltas:
        copy.start()

    def query_grad(h):
        dots = nt(dowin[h, mid], vwin[h])
        grad_scores = (probs[h] * (dots - delta[h]) * scale).astype(BF16)
        gq_v[:, cols(h)] = nn(grad_scores, kwin[h]).astype(BF16)

    def key_grad(h, span):
        prob_t = probs_t[h, :, span]
        d_value = nn(prob_t.astype(BF16), dowin[h, span])
        dots_t = nt(vwin[h, mid], dowin[h, span])
        grad_t = (prob_t * (dots_t - deltawin[h : h + 1, span]) * scale).astype(BF16)
        return nn(grad_t, qwin[h, span]), d_value

    for h in range(heads):
        query_grad(h)
    stores.append(pltpu.make_async_copy(gq_v, gq_hbm, out_sem.at[2]))
    stores[-1].start()
    for n, (one, two) in enumerate(zip(ups, second_ups)):
        one.wait_recv()
        if n < 2:
            two.start()
    for copy in deltas:
        copy.wait_recv()

    for copy in queries[2:] + totals:
        copy.wait_recv()
    for h in range(heads):
        scores_t = nt(kwin[h, mid], qwin[h]) * scale
        probs_t[h] = jnp.where(valid, jnp.exp(scores_t - lsewin[h : h + 1]), 0.0)
    near = slice(frames, 4 * frames)
    for h in range(heads):
        gk_sum[:, cols(h)], gv_sum[:, cols(h)] = key_grad(h, near)
    for copy in second_ups:
        copy.wait_recv()
    for h in range(heads):
        low_k, low_v = key_grad(h, block(0))
        high_k, high_v = key_grad(h, block(4))
        gk_v[:, cols(h)] = (gk_sum[:, cols(h)] + low_k + high_k).astype(BF16)
        gv_v[:, cols(h)] = (gv_sum[:, cols(h)] + low_v + high_v).astype(BF16)
    stores.append(pltpu.make_async_copy(gk_v, gk_hbm, out_sem.at[3]))
    stores[-1].start()
    stores.append(pltpu.make_async_copy(gv_v, gv_hbm, out_sem.at[4]))
    stores[-1].start()

    for copy in list(first.values()) + list(second.values()) + early + shares + queries + totals:
        copy.wait_send()
    for copy in ups + second_ups + deltas:
        copy.wait_send()
    for group in parts + [rims] + [piece[1:] for piece in spread]:
        for copy in group:
            copy.wait_send()
    for copy in stores:
        copy.wait()


def copy_out(*refs):
    sources, targets, held, sems = refs[:5], refs[5:10], refs[10], refs[11]
    half = held.shape[1] // 2
    cuts = [(i, slice(j * half, (j + 1) * half)) for i in range(5) for j in range(2)]
    taken = [
        pltpu.make_async_copy(sources[i].at[at], held.at[i, at], sems.at[0, n]) for n, (i, at) in enumerate(cuts)
    ]
    given = [
        pltpu.make_async_copy(held.at[i, at], targets[i].at[at], sems.at[1, n]) for n, (i, at) in enumerate(cuts)
    ]
    for copy in taken:
        copy.start()
    for one, two in zip(taken, given):
        one.wait()
        two.start()
    for copy in given:
        copy.wait()


def per_device(query_rows, key_rows, value_rows, inputs, out_weight, kernel, cotangent):
    frames, width = query_rows.shape
    heads = width // HDIM
    count = lax.axis_size("ctx")
    window = BLOCKS * frames
    full = out_weight.shape[1]
    chunks = width // HDIM
    taps = kernel.shape[0]
    dma = pltpu.SemaphoreType.DMA
    win = pltpu.VMEM((heads, window, HDIM), BF16)
    scratch = [
        win, win, win, win,
        pltpu.VMEM((8, window), F32),
        pltpu.VMEM((8, window), F32),
        pltpu.VMEM((heads, frames, window), F32),
        pltpu.VMEM((heads, frames, window), F32),
        pltpu.VMEM((2, frames, width), BF16),
        pltpu.VMEM((width, full), BF16),
        pltpu.VMEM((2, width, width), BF16),
        pltpu.VMEM((taps, width), F32),
        pltpu.VMEM((frames, width), BF16),
        pltpu.VMEM((frames + 2 * HALF, width), BF16),
        pltpu.VMEM((frames, width), F32),
        pltpu.VMEM((frames, width), BF16),
        pltpu.VMEM((frames, width), BF16),
        pltpu.VMEM((2, RIM, width), BF16),
        pltpu.VMEM((2, RIM, width), BF16),
        pltpu.VMEM((chunks, frames + 2 * RIM, HDIM), F32),
        pltpu.VMEM((chunks, frames + 2 * HALF, HDIM), F32),
        pltpu.VMEM((4, frames, width), BF16),
        pltpu.VMEM((frames, width), BF16),
        pltpu.VMEM((frames, width), BF16),
        pltpu.VMEM((frames, width), BF16),
        pltpu.VMEM((frames, width), BF16),
        pltpu.VMEM((frames, width), F32),
        pltpu.VMEM((frames, width), F32),
        dma((3 * heads + 4,)),
        dma((5,)),
        dma((4, 2, heads)), dma((4, 2, heads)),
        dma((4,)), dma((4,)),
        dma((4,)), dma((4,)),
        dma((4, heads)), dma((4, heads)),
        dma((4,)), dma((4,)),
        dma((2,)), dma((2,)),
        dma((2,)), dma((2,)),
        dma((heads,)), dma((heads,)),
        dma((chunks,)), dma((chunks,)),
        dma((2,)), dma((2,)),
        dma((3, 4)), dma((3, 4)),
    ]
    shape = jax.ShapeDtypeStruct((frames, width), BF16)
    results = pl.pallas_call(
        functools.partial(kernel_body, count, heads),
        out_shape=(shape,) * 5,
        in_specs=[pl.BlockSpec(memory_space=pl.ANY)] * 7,
        out_specs=(pl.BlockSpec(memory_space=pl.ANY),) * 5,
        scratch_shapes=scratch,
        compiler_params=pltpu.CompilerParams(
            collective_id=0, has_side_effects=True, vmem_limit_bytes=56 * 1024 * 1024
        ),
        name="conformer",
    )(query_rows, key_rows, value_rows, inputs, out_weight, kernel, cotangent)
    return pl.pallas_call(
        copy_out,
        out_shape=(shape,) * 5,
        in_specs=[pl.BlockSpec(memory_space=pl.ANY)] * 5,
        out_specs=(pl.BlockSpec(memory_space=pl.ANY),) * 5,
        scratch_shapes=[pltpu.VMEM((5, frames, width), BF16), dma((2, 10))],
        compiler_params=pltpu.CompilerParams(vmem_limit_bytes=56 * 1024 * 1024),
        name="copy_out",
    )(*results)


def solution(mesh):
    placed = (
        P("ctx", "mp"),
        P("ctx", "mp"),
        P("ctx", "mp"),
        P("ctx", "mp"),
        P("mp", None),
        P(None, "mp"),
        P("ctx", "mp"),
    )
    return jax.shard_map(
        per_device,
        mesh=mesh,
        in_specs=placed,
        out_specs=(P("ctx", "mp"),) * 5,
        check_vma=False,
    )
```

```python
import functools
import math

import jax
import jax.numpy as jnp
from jax import lax
from jax.experimental import pallas as pl
from jax.experimental.pallas import tpu as pltpu
from jax.sharding import PartitionSpec as P

HDIM = 128
LOOK = 2
BLOCKS = 2 * LOOK + 1
RIM = 32
HALF = 16
MESH = pl.DeviceIdType.MESH
F32 = jnp.float32
BF16 = jnp.bfloat16


def nt(a, b):
    return lax.dot_general(a, b, (((1,), (1,)), ((), ())), preferred_element_type=F32)


def nn(a, b):
    return jnp.dot(a, b, preferred_element_type=F32)


def kernel_body(
    count,
    heads,
    q_hbm,
    k_hbm,
    v_hbm,
    in_hbm,
    w_hbm,
    tap_hbm,
    cot_hbm,
    out_hbm,
    gi_hbm,
    gq_hbm,
    gk_hbm,
    gv_hbm,
    qwin,
    kwin,
    vwin,
    dowin,
    lsewin,
    deltawin,
    probs,
    probs_t,
    att,
    w_own,
    w_sib,
    taps,
    inp,
    cotp,
    own_sum,
    part_send,
    part_recv,
    rim_send,
    rim_own,
    hpad,
    gpad,
    gfull,
    out_v,
    gq_v,
    gk_v,
    gv_v,
    gk_sum,
    gv_sum,
    local_sem,
    out_sem,
    kv_send,
    kv_recv,
    q_send,
    q_recv,
    lse_send,
    lse_recv,
    do_send,
    do_recv,
    delta_send,
    delta_recv,
    w_send,
    w_recv,
    cot_send,
    cot_recv,
    att_send,
    att_recv,
    part_ssem,
    part_rsem,
    rim_ssem,
    rim_rsem,
    gi_send,
    gi_recv,
):
    frames, width = inp.shape
    ntaps = taps.shape[0]
    scale = 1.0 / math.sqrt(HDIM)
    c = lax.axis_index("ctx")
    m = lax.axis_index("mp")
    right = lax.rem(c + 1, count)
    right2 = lax.rem(c + 2, count)
    left = lax.rem(c + count - 1, count)
    left2 = lax.rem(c + count - 2, count)
    sib_m = m + 1 - 2 * lax.rem(m, 2)
    far_m = lax.rem(m + 2, 4)
    far_sib_m = lax.rem(sib_m + 2, 4)
    sib = (c, sib_m)
    far = (c, far_m)

    barrier = pltpu.get_barrier_semaphore()
    exists = [c < count - 1, c > 0, c < count - 2, c > 1]
    targets = [right, left, right2, left2]
    places = [1, 3, 0, 4]

    def toward(i, plane=None):
        other = sib_m if plane is None else plane
        own = m if plane is None else plane
        return (jnp.where(exists[i], targets[i], c), jnp.where(exists[i], own, other))

    def turned(i, value, mirrored):
        return jnp.where(exists[i], value, mirrored)

    def place(i, slot):
        return pl.ds(pl.multiple_of(turned(i, slot, 4 - slot) * frames, frames), frames)

    partners = [toward(i) for i in range(4)] + [sib, far]
    for device in partners:
        pl.semaphore_signal(barrier, inc=1, device_id=device, device_id_type=MESH)

    def local(src, dst, at):
        copy = pltpu.make_async_copy(src, dst, local_sem.at[at])
        copy.start()
        return copy

    def remote(src, dst, send, recv, device):
        return pltpu.make_async_remote_copy(
            src_ref=src, dst_ref=dst, send_sem=send, recv_sem=recv,
            device_id=device, device_id_type=MESH,
        )

    class Crossing:
        def __init__(self, sent, due):
            self.start, self.wait_send, self.wait_recv = sent.start, sent.wait_send, due.wait_recv

    def shift(src, dst, due_dst, send, recv, due_recv, device):
        return Crossing(
            remote(src, dst, send, recv, device), remote(src, due_dst, send, due_recv, device)
        )

    def cols(index):
        return slice(index * HDIM, (index + 1) * HDIM)

    def block(slot):
        return slice(slot * frames, (slot + 1) * frames)

    def wide(index):
        return pl.ds(pl.multiple_of(index * width, width), width)

    mid = block(LOOK)
    pl.semaphore_wait(barrier, len(partners))

    first = {}
    second = {}
    for h in range(heads):
        for i, (src, win) in enumerate(((k_hbm, kwin), (v_hbm, vwin))):
            for side in range(2):
                near_slot, far_slot = places[side], places[2 + side]
                first[h, i, side] = shift(
                    src.at[:, cols(h)], win.at[h, place(side, near_slot)], win.at[h, block(near_slot)],
                    kv_send.at[side, i, h], kv_recv.at[turned(side, side, 1 - side), i, h],
                    kv_recv.at[side, i, h], toward(side),
                )
                first[h, i, side].start()
                if h == heads - 1:
                    over = 2 + side
                    second[h, i, side] = shift(
                        src.at[:, cols(h)], win.at[h, place(over, far_slot)], win.at[h, block(far_slot)],
                        kv_send.at[over, i, h], kv_recv.at[turned(over, over, over ^ 1), i, h],
                        kv_recv.at[over, i, h], toward(over),
                    )
                    second[h, i, side].start()
                    continue
                second[h, i, side] = shift(
                    win.at[h, block(near_slot)], win.at[h, place(side, far_slot)], win.at[h, block(far_slot)],
                    kv_send.at[2 + side, i, h], kv_recv.at[2 + turned(side, side, 1 - side), i, h],
                    kv_recv.at[2 + side, i, h], toward(side),
                )

    early = [
        remote(w_hbm.at[:, wide(sib_m)], w_sib.at[0], w_send.at[0], w_recv.at[0], sib),
        remote(w_hbm.at[:, wide(far_sib_m)], w_sib.at[1], w_send.at[1], w_recv.at[1], sib),
    ]
    cot_starts = (0, HALF + frames)
    for side, rows in enumerate((slice(frames - HALF, frames), slice(0, HALF))):
        start = turned(side, cot_starts[side], cot_starts[1 - side])
        early.append(shift(
            cot_hbm.at[rows], cotp.at[pl.ds(pl.multiple_of(start, HALF), HALF)],
            cotp.at[cot_starts[side] : cot_starts[side] + HALF],
            cot_send.at[side], cot_recv.at[turned(side, side, 1 - side)], cot_recv.at[side], toward(side),
        ))
    loads = {}
    for h in range(heads):
        loads["q", h] = local(q_hbm.at[:, cols(h)], qwin.at[h, mid], h)
        loads["k", h] = local(k_hbm.at[:, cols(h)], kwin.at[h, mid], heads + h)
        loads["v", h] = local(v_hbm.at[:, cols(h)], vwin.at[h, mid], 2 * heads + h)
    at = 3 * heads
    loads["w"] = local(w_hbm, w_own, at)
    loads["taps"] = local(tap_hbm, taps, at + 1)
    loads["inp"] = local(in_hbm, inp, at + 2)
    loads["cot"] = local(cot_hbm, cotp.at[HALF : HALF + frames], at + 3)

    for h in range(heads):
        for side in range(2):
            for i in range(2):
                first[h, i, side].wait_recv()
                if h < heads - 1:
                    second[h, i, side].start()

    for copy in early:
        copy.start()

    owner = lax.shift_right_logical(
        lax.broadcasted_iota(jnp.int32, (1, BLOCKS * frames), 1), 7
    ) + c
    valid = (owner >= LOOK) & (owner < count + LOOK)
    lane = lax.broadcasted_iota(jnp.int32, (frames, HDIM), 1)

    def spread_to(i, win, send, recv, source=mid):
        return shift(
            win.at[:, source], win.at[:, place(i, places[i])], win.at[:, block(places[i])],
            send.at[i], recv.at[turned(i, i, i ^ 1)], recv.at[i], toward(i),
        )

    def relay_to(side, win, send, recv):
        near_slot, far_slot = places[side], places[2 + side]
        return shift(
            win.at[:, block(near_slot)], win.at[:, place(side, far_slot)], win.at[:, block(far_slot)],
            send.at[2 + side], recv.at[2 + turned(side, side, 1 - side)], recv.at[2 + side], toward(side),
        )

    queries = [spread_to(side, qwin, q_send, q_recv) for side in range(2)]
    queries += [relay_to(side, qwin, q_send, q_recv) for side in range(2)]

    stat = jnp.zeros((frames, HDIM), F32)
    shares = []
    for h in range(heads):
        loads["q", h].wait()
        loads["k", h].wait()
        loads["v", h].wait()
        for side in range(2):
            for i in range(2):
                second[h, i, side].wait_recv()
        if h == heads - 1:
            queries[0].start()
            queries[1].start()
        scores = nt(qwin[h, mid], kwin[h]) * scale
        scores = jnp.where(valid, scores, -jnp.inf)
        top = jnp.max(scores, axis=1, keepdims=True)
        weights = jnp.exp(scores - top)
        total = jnp.sum(weights, axis=1, keepdims=True)
        stat = jnp.where(lane == h, top + jnp.log(total), stat)
        prob = weights * (1.0 / total)
        probs[h] = prob
        att[0, :, cols(h)] = nn(prob.astype(BF16), vwin[h]).astype(BF16)
        share = remote(att.at[0, :, cols(h)], att.at[1, :, cols(h)], att_send.at[h], att_recv.at[h], sib)
        share.start()
        shares.append(share)

    loads["w"].wait()
    far_part = nn(att[0], w_own[:, wide(far_m)])
    lsewin[:, mid] = jnp.transpose(stat)[0:8]
    early[0].wait_recv()
    early[1].wait_recv()
    for share in shares:
        share.wait_recv()
    parts = []
    for j in range(width // HDIM):
        lanes = cols(j)
        part_send[:, lanes] = (far_part[:, lanes] + nn(att[1], w_sib[1, :, lanes])).astype(BF16)
        group = [
            remote(part_send.at[:, lanes], part_recv.at[:, lanes], part_ssem.at[j], part_rsem.at[j], far)
        ]
        for copy in group:
            copy.start()
        parts.append(group)
    loads["inp"].wait()
    own_part = nn(att[0], w_own[:, wide(m)])
    summed = own_part + nn(att[1], w_sib[0]) + inp[...].astype(F32)
    own_sum[...] = summed

    totals = [spread_to(i, lsewin, lse_send, lse_recv) for i in range(4)]
    for copy in totals:
        copy.start()

    loads["taps"].wait()
    loads["cot"].wait()
    early[2].wait_recv()
    early[3].wait_recv()

    row = lax.broadcasted_iota(jnp.int32, (frames + 2 * HALF, HDIM), 0)
    inside = ((row >= HALF) | (c > 0)) & ((row < HALF + frames) | (c < count - 1))
    for j in range(width // HDIM):
        lanes = cols(j)
        for copy in parts[j]:
            copy.wait_recv()
        hidden = (own_sum[:, lanes] + part_recv[:, lanes].astype(F32)).astype(BF16)
        hpad[j, RIM : RIM + frames] = hidden.astype(F32)
        rim_send[0, :, lanes] = hidden[frames - RIM : frames]
        rim_send[1, :, lanes] = hidden[0:RIM]
    rims = []
    for side in range(2):
        turn = turned(side, side, 1 - side)
        rims.append(shift(
            rim_send.at[side], rim_own.at[turn], rim_own.at[side],
            rim_ssem.at[side], rim_rsem.at[turn], rim_rsem.at[side], toward(side),
        ))
        rims[-1].start()

    def conv_rows(j, start, rows):
        lanes = cols(j)
        conv = jnp.zeros((rows, HDIM), F32)
        for tap in range(ntaps):
            at = start + RIM - HALF + 1 + tap
            conv = conv + taps[tap : tap + 1, lanes] * hpad[j, at : at + rows]
        gate = jax.nn.sigmoid(conv)
        swish = conv * gate
        low, high = max(start, 0), min(start + rows, frames)
        out_v[low:high, lanes] = (
            hpad[j, RIM + low : RIM + high] + swish[low - start : high - start]
        ).astype(BF16)
        span = slice(start + HALF, start + HALF + rows)
        cot = cotp[span, lanes].astype(F32)
        grad_conv = (cot * (gate + swish * (1.0 - gate))).astype(BF16).astype(F32)
        gpad[j, span] = jnp.where(inside[span], grad_conv, 0.0)

    def grad_rows(j, start, rows):
        lanes = cols(j)
        grad = cotp[HALF + start : HALF + start + rows, lanes].astype(F32)
        for tap in range(ntaps):
            at = start + 2 * HALF - 1 - tap
            grad = grad + taps[tap : tap + 1, lanes] * gpad[j, at : at + rows]
        gfull[0, start : start + rows, lanes] = grad.astype(BF16)

    edges = ((0, RIM), (frames - RIM, RIM))
    spans = (((RIM, frames - 2 * RIM),), edges)
    spread = []

    def leave(part, start, rows, lanes):
        at, n = slice(start, start + rows), len(spread)
        pieces = (
            remote(gfull.at[0, at, lanes], gfull.at[1, at, lanes], gi_send.at[0, n], gi_recv.at[0, n], sib),
            remote(gfull.at[0, at, lanes], gfull.at[2, at, lanes], gi_send.at[1, n], gi_recv.at[1, n], far),
            remote(gfull.at[2, at, lanes], gfull.at[3, at, lanes], gi_send.at[2, n], gi_recv.at[2, n], sib),
        )
        pieces[1].start()
        pieces[0].start()
        spread.append((part,) + pieces)

    for j in range(width // HDIM):
        conv_rows(j, HALF, frames - 2 * HALF)
        grad_rows(j, RIM, frames - 2 * RIM)
        if j % 2 == 1:
            leave(0, RIM, frames - 2 * RIM, slice((j - 1) * HDIM, (j + 1) * HDIM))
    for copy in rims:
        copy.wait_recv()
    for j in range(width // HDIM):
        lanes = cols(j)
        hpad[j, 0:RIM] = jnp.where(c > 0, rim_own[0, :, lanes].astype(F32), 0.0)
        hpad[j, RIM + frames : 2 * RIM + frames] = jnp.where(c < count - 1, rim_own[1, :, lanes].astype(F32), 0.0)
        conv_rows(j, -HALF, 2 * HALF)
        conv_rows(j, frames - HALF, 2 * HALF)
        for start, rows in edges:
            grad_rows(j, start, rows)
    for start, rows in edges:
        leave(1, start, rows, slice(0, width))

    stores = [
        pltpu.make_async_copy(out_v, out_hbm, out_sem.at[0]),
        pltpu.make_async_copy(gfull.at[0], gi_hbm, out_sem.at[1]),
    ]
    for copy in stores:
        copy.start()

    for side in range(2):
        queries[side].wait_recv()
        queries[2 + side].start()

    ups = []
    second_ups = []
    def rows_of(take, part):
        pieces = [take(slice(start, start + rows)) for start, rows in spans[part]]
        return pieces[0] if len(pieces) == 1 else jnp.concatenate(pieces, axis=0)

    for r in range(2):
        mine = [piece for piece in spread if piece[0] == r]
        up = nt(rows_of(lambda at: gfull[0, at], r), w_own[:, wide(m)])
        for _, to_sib, _, _ in mine:
            to_sib.wait_recv()
        up = up + nt(rows_of(lambda at: gfull[1, at], r), w_own[:, wide(sib_m)])
        for _, _, to_far, relay in mine:
            to_far.wait_recv()
            relay.start()
        up = up + nt(rows_of(lambda at: gfull[2, at], r), w_own[:, wide(far_m)])
        for _, _, _, relay in mine:
            relay.wait_recv()
        up = up + nt(rows_of(lambda at: gfull[3, at], r), w_own[:, wide(far_sib_m)])
        upstream = up.astype(BF16)
        begun = 0
        for start, rows in spans[r]:
            for h in range(heads):
                dowin[h, LOOK * frames + start : LOOK * frames + start + rows] = upstream[begun : begun + rows, cols(h)]
            begun += rows

        for start, rows in spans[r]:
            n = len(ups) // 2

            def rows_at(slot, start=start, rows=rows):
                return pl.ds(pl.multiple_of(slot * frames + start, RIM), rows)

            for side in range(2):
                turn = turned(side, side, 1 - side)
                near_slot, far_slot = places[side], places[2 + side]
                own_at, near_at, far_at = rows_at(LOOK), rows_at(near_slot), rows_at(far_slot)
                near_to = rows_at(turned(side, near_slot, 4 - near_slot))
                far_to = rows_at(turned(side, far_slot, 4 - far_slot))
                ups.append(shift(
                    dowin.at[:, own_at], dowin.at[:, near_to], dowin.at[:, near_at],
                    do_send.at[side, n], do_recv.at[turn, n], do_recv.at[side, n], toward(side),
                ))
                ups[-1].start()
                if r == 0:
                    second_ups.append(shift(
                        dowin.at[:, near_at], dowin.at[:, far_to], dowin.at[:, far_at],
                        do_send.at[2 + side, n], do_recv.at[2 + turn, n], do_recv.at[2 + side, n], toward(side),
                    ))
                    continue
                over = 2 + side
                far_to = rows_at(turned(over, far_slot, 4 - far_slot))
                second_ups.append(shift(
                    dowin.at[:, own_at], dowin.at[:, far_to], dowin.at[:, far_at],
                    do_send.at[over, n], do_recv.at[turned(over, over, over ^ 1), n], do_recv.at[over, n], toward(over),
                ))
                second_ups[-1].start()

    delta = []
    stat = jnp.zeros((frames, HDIM), F32)
    for h in range(heads):
        delta.append(
            jnp.sum(dowin[h, mid].astype(F32) * att[0, :, cols(h)].astype(F32), axis=1, keepdims=True)
        )
        stat = jnp.where(lane == h, delta[h], stat)
    deltawin[:, mid] = jnp.transpose(stat)[0:8]
    deltas = [spread_to(i, deltawin, delta_send, delta_recv) for i in range(4)]
    for copy in deltas:
        copy.start()

    def query_grad(h):
        dots = nt(dowin[h, mid], vwin[h])
        grad_scores = (probs[h] * (dots - delta[h]) * scale).astype(BF16)
        gq_v[:, cols(h)] = nn(grad_scores, kwin[h]).astype(BF16)

    def key_grad(h, span):
        prob_t = probs_t[h, :, span]
        d_value = nn(prob_t.astype(BF16), dowin[h, span])
        dots_t = nt(vwin[h, mid], dowin[h, span])
        grad_t = (prob_t * (dots_t - deltawin[h : h + 1, span]) * scale).astype(BF16)
        return nn(grad_t, qwin[h, span]), d_value

    for h in range(heads):
        query_grad(h)
    stores.append(pltpu.make_async_copy(gq_v, gq_hbm, out_sem.at[2]))
    stores[-1].start()
    for n, (one, two) in enumerate(zip(ups, second_ups)):
        one.wait_recv()
        if n < 2:
            two.start()
    for copy in deltas:
        copy.wait_recv()

    for copy in queries[2:] + totals:
        copy.wait_recv()
    for h in range(heads):
        scores_t = nt(kwin[h, mid], qwin[h]) * scale
        probs_t[h] = jnp.where(valid, jnp.exp(scores_t - lsewin[h : h + 1]), 0.0)
    near = slice(frames, 4 * frames)
    for h in range(heads):
        gk_sum[:, cols(h)], gv_sum[:, cols(h)] = key_grad(h, near)
    for copy in second_ups:
        copy.wait_recv()
    for h in range(heads):
        low_k, low_v = key_grad(h, block(0))
        high_k, high_v = key_grad(h, block(4))
        gk_v[:, cols(h)] = (gk_sum[:, cols(h)] + low_k + high_k).astype(BF16)
        gv_v[:, cols(h)] = (gv_sum[:, cols(h)] + low_v + high_v).astype(BF16)
    stores.append(pltpu.make_async_copy(gk_v, gk_hbm, out_sem.at[3]))
    stores[-1].start()
    stores.append(pltpu.make_async_copy(gv_v, gv_hbm, out_sem.at[4]))
    stores[-1].start()

    for copy in list(first.values()) + list(second.values()) + early + shares + queries + totals:
        copy.wait_send()
    for copy in ups + second_ups + deltas:
        copy.wait_send()
    for group in parts + [rims] + [piece[1:] for piece in spread]:
        for copy in group:
            copy.wait_send()
    for copy in stores:
        copy.wait()


def copy_out(*refs):
    sources, targets, held, sems = refs[:5], refs[5:10], refs[10], refs[11]
    half = held.shape[1] // 2
    cuts = [(i, slice(j * half, (j + 1) * half)) for i in range(5) for j in range(2)]
    taken = [
        pltpu.make_async_copy(sources[i].at[at], held.at[i, at], sems.at[0, n]) for n, (i, at) in enumerate(cuts)
    ]
    given = [
        pltpu.make_async_copy(held.at[i, at], targets[i].at[at], sems.at[1, n]) for n, (i, at) in enumerate(cuts)
    ]
    for copy in taken:
        copy.start()
    for one, two in zip(taken, given):
        one.wait()
        two.start()
    for copy in given:
        copy.wait()


def per_device(query_rows, key_rows, value_rows, inputs, out_weight, kernel, cotangent):
    frames, width = query_rows.shape
    heads = width // HDIM
    count = lax.axis_size("ctx")
    window = BLOCKS * frames
    full = out_weight.shape[1]
    chunks = width // HDIM
    taps = kernel.shape[0]
    dma = pltpu.SemaphoreType.DMA
    win = pltpu.VMEM((heads, window, HDIM), BF16)
    scratch = [
        win, win, win, win,
        pltpu.VMEM((8, window), F32),
        pltpu.VMEM((8, window), F32),
        pltpu.VMEM((heads, frames, window), F32),
        pltpu.VMEM((heads, frames, window), F32),
        pltpu.VMEM((2, frames, width), BF16),
        pltpu.VMEM((width, full), BF16),
        pltpu.VMEM((2, width, width), BF16),
        pltpu.VMEM((taps, width), F32),
        pltpu.VMEM((frames, width), BF16),
        pltpu.VMEM((frames + 2 * HALF, width), BF16),
        pltpu.VMEM((frames, width), F32),
        pltpu.VMEM((frames, width), BF16),
        pltpu.VMEM((frames, width), BF16),
        pltpu.VMEM((2, RIM, width), BF16),
        pltpu.VMEM((2, RIM, width), BF16),
        pltpu.VMEM((chunks, frames + 2 * RIM, HDIM), F32),
        pltpu.VMEM((chunks, frames + 2 * HALF, HDIM), F32),
        pltpu.VMEM((4, frames, width), BF16),
        pltpu.VMEM((frames, width), BF16),
        pltpu.VMEM((frames, width), BF16),
        pltpu.VMEM((frames, width), BF16),
        pltpu.VMEM((frames, width), BF16),
        pltpu.VMEM((frames, width), F32),
        pltpu.VMEM((frames, width), F32),
        dma((3 * heads + 4,)),
        dma((5,)),
        dma((4, 2, heads)), dma((4, 2, heads)),
        dma((4,)), dma((4,)),
        dma((4,)), dma((4,)),
        dma((4, heads)), dma((4, heads)),
        dma((4,)), dma((4,)),
        dma((2,)), dma((2,)),
        dma((2,)), dma((2,)),
        dma((heads,)), dma((heads,)),
        dma((chunks,)), dma((chunks,)),
        dma((2,)), dma((2,)),
        dma((3, 4)), dma((3, 4)),
    ]
    shape = jax.ShapeDtypeStruct((frames, width), BF16)
    results = pl.pallas_call(
        functools.partial(kernel_body, count, heads),
        out_shape=(shape,) * 5,
        in_specs=[pl.BlockSpec(memory_space=pl.ANY)] * 7,
        out_specs=(pl.BlockSpec(memory_space=pl.ANY),) * 5,
        scratch_shapes=scratch,
        compiler_params=pltpu.CompilerParams(
            collective_id=0, has_side_effects=True, vmem_limit_bytes=56 * 1024 * 1024
        ),
        name="conformer",
    )(query_rows, key_rows, value_rows, inputs, out_weight, kernel, cotangent)
    return pl.pallas_call(
        copy_out,
        out_shape=(shape,) * 5,
        in_specs=[pl.BlockSpec(memory_space=pl.ANY)] * 5,
        out_specs=(pl.BlockSpec(memory_space=pl.ANY),) * 5,
        scratch_shapes=[pltpu.VMEM((5, frames, width), BF16), dma((2, 10))],
        compiler_params=pltpu.CompilerParams(vmem_limit_bytes=56 * 1024 * 1024),
        name="copy_out",
    )(*results)


def solution(mesh):
    placed = (
        P("ctx", "mp"),
        P("ctx", "mp"),
        P("ctx", "mp"),
        P("ctx", "mp"),
        P("mp", None),
        P(None, "mp"),
        P("ctx", "mp"),
    )
    return jax.shard_map(
        per_device,
        mesh=mesh,
        in_specs=placed,
        out_specs=(P("ctx", "mp"),) * 5,
        check_vma=False,
    )
```
